32 devices in a mesh: chan: 4 (over z), win: 8 (over y, x, core).
Axes of the slice: x: 2, y: 2, z: 4, core: 2. Of those that a mesh axis runs over, the one named last changes fastest.
Arguments:
- records: bfloat16 [1024, 81920], P('chan', 'win'), may hold values from -50 to 50
- fir_taps: float32 [64], replicated, may hold values from -0.75 to 0.75
- plan: int32 [2, 4], replicated, may hold values from 0 to 3, as said below
Outputs:
- cross: float32 [64, 2, 2, 256, 1024], P('win', None, None, None, 'chan')
The draws below stay inside these ranges and needn't reach their ends.
Inputs may be any that keep to these rules, and one draw needn't show every extreme that they name: `plan`: in each round block c is paired with block c XOR k for one nonzero key k, the same k for all blocks of the round; the rounds use different keys.
All inputs are finite; a program needn't handle non-finite values.
Results may differ from the reference program's by a relative error of at most 0.02.
Values may be sent and summed in bfloat16 or wider, within the bound.
A program may use at most 128 MiB of HBM per device.

```python
import math
from functools import partial
import jax
import jax.numpy as jnp
from jax import lax

CB = 256
WL = 256
F = 64
TAPS = 64
ROUNDS = 2
WIN_DEV = 40
BLOCKS = 4
NCH = 1024
WINDOWS = 320
TIME = 81920
N_WIN = 8


def draw_records(key, part):
    noise_key, scale_key = jax.random.split(jax.random.fold_in(key, 11), 2)
    gains = jnp.exp(jax.random.uniform(scale_key, (NCH, 1), jnp.float32) * math.log(10.0))
    noise = jnp.clip(jax.random.normal(noise_key, (NCH, TIME), jnp.float32), -5.0, 5.0)
    values = noise * gains
    return values.astype(jnp.bfloat16)


def draw_plan(key, part):
    first_key, second_key = jax.random.split(jax.random.fold_in(key, 29))
    first_pick = jax.random.randint(first_key, (), 1, BLOCKS, dtype=jnp.int32)
    second_pick = (first_pick - 1 + jax.random.randint(second_key, (), 1, BLOCKS - 1, dtype=jnp.int32)) % (BLOCKS - 1) + 1
    round_keys = jnp.stack([first_pick, second_pick]).astype(jnp.int32)
    block_numbers = jnp.arange(BLOCKS, dtype=jnp.int32)
    return jnp.bitwise_xor(block_numbers[None, :], round_keys[:, None]).astype(jnp.int32)


def bell_draw(stream_key, extent, width, bound, held_as=jnp.bfloat16):
    entries = jax.random.normal(stream_key, extent, jnp.float32) * width
    return jnp.minimum(jnp.maximum(entries, -bound), bound).astype(held_as)


def setup_inputs(seed: int = 0) -> dict:
    keys = jax.random.split(jax.random.key(seed), 4)
    return {
        "records": draw_records(jax.random.fold_in(keys[3], 71), 0),
        "fir_taps": bell_draw(keys[1], (TAPS,), 0.125, 0.75, jnp.float32),
        "plan": draw_plan(jax.random.fold_in(keys[3], 71), 0),
    }


def fir_matrix(fir_taps):
    inputs_at = jnp.arange(WL + TAPS - 1, dtype=jnp.int32)[:, None]
    outputs_at = jnp.arange(WL, dtype=jnp.int32)[None, :]
    tap_number = outputs_at + (TAPS - 1) - inputs_at
    inside = (tap_number >= 0) & (tap_number < TAPS)
    picked = fir_taps[jnp.clip(tap_number, 0, TAPS - 1)]
    return jnp.where(inside, picked, jnp.zeros_like(picked))

def whiten_block(block_rows, fir_taps):
    channels = block_rows.shape[0]
    samples = block_rows.astype(jnp.float32).reshape(channels, WINDOWS, WL)
    leading = jnp.zeros((channels, 1, TAPS - 1), samples.dtype)
    previous = jnp.concatenate([leading, samples[:, :-1, WL - TAPS + 1:]], axis=1)
    extended = jnp.concatenate([previous, samples], axis=2)
    filtered = jnp.einsum('cwi,in->cwn', extended, fir_matrix(fir_taps), precision=lax.Precision.HIGHEST)
    spectrum = jnp.fft.rfft(filtered, axis=-1)[:, :, 1:F + 1]
    stacked = jnp.concatenate([jnp.real(spectrum), jnp.imag(spectrum)], axis=-1).astype(jnp.float32)
    band_power = lax.optimization_barrier(jnp.mean(stacked * stacked, axis=-1, keepdims=True)) + 1e-06
    return (stacked / jnp.sqrt(band_power)).astype(jnp.bfloat16)

def arrange(whitened):
    channels, windows_here, doubled = whitened.shape
    return whitened.reshape(channels, windows_here, 2, doubled // 2).transpose(3, 0, 2, 1)

def stack_partners(partner_list):
    layers = []
    for arranged in partner_list:
        rotated = jnp.stack([-arranged[:, :, 1], arranged[:, :, 0]], axis=2)
        layers.append(jnp.stack([arranged, rotated], axis=1))
    joined = jnp.stack(layers, axis=1)
    bins_here, rounds_here, halves, channels, components, windows_here = joined.shape
    return joined.reshape(bins_here, rounds_here * halves * channels, components, windows_here)

def block_cross(block_index, whitened, plan):
    own_rows = arrange(whitened[block_index])
    partner_list = [arrange(whitened[plan[round_index, block_index]]) for round_index in range(ROUNDS)]
    partner_rows = stack_partners(partner_list)
    own_groups = own_rows.reshape(F, CB, 2, N_WIN, WIN_DEV).transpose(3, 0, 1, 2, 4).reshape(N_WIN, F, CB, 2 * WIN_DEV)
    partner_groups = partner_rows.reshape(F, ROUNDS * 2 * CB, 2, N_WIN, WIN_DEV).transpose(3, 0, 1, 2, 4).reshape(N_WIN, F, ROUNDS * 2 * CB, 2 * WIN_DEV)
    scale = 1.0 / math.sqrt(WINDOWS)

    def add_group(running, pieces):
        own_piece, partner_piece = pieces
        product = jnp.einsum('fjk,fak->fja', partner_piece.astype(jnp.float32), own_piece.astype(jnp.float32)) * scale
        rounded = lax.optimization_barrier(product.astype(jnp.bfloat16))
        return (running + rounded.astype(jnp.float32), None)
    start_sum = jnp.zeros((F, ROUNDS * 2 * CB, CB), jnp.float32)
    summed, ignored = lax.scan(add_group, start_sum, (own_groups, partner_groups))
    return summed

def reference(records, fir_taps, plan):
    blocks_in = records.reshape(BLOCKS, CB, TIME)
    whitened = lax.map(partial(whiten_block, fir_taps=fir_taps), blocks_in)
    per_block = lax.map(partial(block_cross, whitened=whitened, plan=plan), jnp.arange(BLOCKS, dtype=jnp.int32))
    shaped = per_block.reshape(BLOCKS, F, ROUNDS, 2, CB, CB).transpose(1, 2, 3, 4, 0, 5)
    return shaped.reshape(F, ROUNDS, 2, CB, NCH)
```

```python
import functools
import math

import jax
import jax.numpy as jnp
from jax import lax
from jax.experimental import pallas as pl
from jax.experimental.pallas import tpu as pltpu
from jax.sharding import PartitionSpec as P

WL = 256
F = 64
TAPS = 64
ROUNDS = 2
MESH = pl.DeviceIdType.MESH


def shifted(array, axis, by):
    count = lax.axis_size(axis)
    pairs = [(i, i + by) for i in range(count) if 0 <= i + by < count]
    return lax.ppermute(array, axis, pairs)


def from_partner(block, axis, bit):
    count = lax.axis_size(axis)
    route = []
    for low in range(count):
        high = low | 1 << bit
        if high != low and high < count:
            route += [(low, high), (high, low)]
    return lax.ppermute(block, axis, route)


def fir_matrix(fir_taps):
    inputs_at = jnp.arange(WL + TAPS - 1, dtype=jnp.int32)[:, None]
    outputs_at = jnp.arange(WL, dtype=jnp.int32)[None, :]
    tap_number = outputs_at + (TAPS - 1) - inputs_at
    inside = (tap_number >= 0) & (tap_number < TAPS)
    picked = fir_taps[jnp.clip(tap_number, 0, TAPS - 1)]
    return jnp.where(inside, picked, jnp.zeros_like(picked))


def dft_table():
    sample_at = jnp.arange(WL, dtype=jnp.int32)[:, None]
    column_at = jnp.arange(2 * F, dtype=jnp.int32)[None, :]
    bin_number = column_at // 2 + 1
    phases = (sample_at * bin_number % WL).astype(jnp.float32) * (2.0 * math.pi / WL)
    return jnp.where(column_at % 2 == 0, jnp.cos(phases), -jnp.sin(phases))


def split_table(fir_taps):
    table = jnp.dot(fir_matrix(fir_taps), dft_table(), precision=lax.Precision.HIGHEST)
    high = table.astype(jnp.bfloat16)
    low = (table - high.astype(jnp.float32)).astype(jnp.bfloat16)
    return jnp.concatenate([high, low], axis=1)


def whiten(records, fir_taps):
    channels, samples_here = records.shape
    window_count = samples_here // WL
    previous_tail = shifted(records[:, samples_here - TAPS + 1 :], "win", 1)
    samples = records.reshape(channels, window_count, WL)
    previous = jnp.concatenate(
        [previous_tail[:, None, :], samples[:, :-1, WL - TAPS + 1 :]], axis=1
    )
    table = split_table(fir_taps)
    both = jnp.einsum(
        "cwi,ik->kwc", samples, table[TAPS - 1 :], preferred_element_type=jnp.float32
    )
    both = both + jnp.einsum(
        "cwi,ik->kwc", previous, table[: TAPS - 1], preferred_element_type=jnp.float32
    )
    stacked = both[: 2 * F] + both[2 * F :]
    band_power = jnp.mean(stacked * stacked, axis=0, keepdims=True) + 1e-06
    return (stacked / jnp.sqrt(band_power)).astype(jnp.bfloat16)


def exchange_kernel(owners, bins, rows, flags, x, gathered, own, recv, stage,
                    a2a_send, a2a_recv, z_send, z_recv, flush_sem):
    chan = lax.axis_index("chan")
    me = lax.axis_index("win")
    is_mid = jnp.logical_and(chan >= 1, chan <= 2)
    is_end = jnp.logical_not(is_mid)
    inner = 3 - chan
    outer = 3 * (chan - 1)
    next_in = 1 + chan // 3

    barrier = pltpu.get_barrier_semaphore()
    for step in range(1, owners):
        pl.semaphore_signal(barrier, inc=1, device_id={"win": lax.rem(me + step, owners)}, device_id_type=MESH)

    @pl.when(is_mid)
    def _():
        pl.semaphore_signal(barrier, inc=1, device_id={"chan": inner}, device_id_type=MESH)
        pl.semaphore_signal(barrier, inc=1, device_id={"chan": outer}, device_id_type=MESH)
        pl.semaphore_wait(barrier, owners + 1)

    @pl.when(is_end)
    def _():
        pl.semaphore_signal(barrier, inc=1, device_id={"chan": next_in}, device_id_type=MESH)
        pl.semaphore_wait(barrier, owners)

    mine = pl.ds(pl.multiple_of(me * rows, rows), rows)

    def start_block(m, carry):
        for step in range(1, owners):
            target = lax.rem(me + step, owners)
            pltpu.make_async_remote_copy(
                src_ref=x.at[target, m], dst_ref=own.at[m, mine],
                send_sem=a2a_send.at[m], recv_sem=a2a_recv.at[m],
                device_id={"win": target}, device_id_type=MESH,
            ).start()
        own[m, mine] = x[me, m]
        return carry

    lax.fori_loop(0, bins, start_block, 0)

    others = pl.ds(0, (owners - 1) * rows)

    def arrived(m):
        pltpu.make_async_copy(own.at[m, others], own.at[m, others], a2a_recv.at[m]).wait()

    def flush(slot, source, m):
        return pltpu.make_async_copy(source.at[m], gathered.at[slot, m], flush_sem.at[slot, m])

    def along(source, slot, m, which, target):
        return pltpu.make_async_remote_copy(
            src_ref=source.at[m], dst_ref=recv.at[slot, m],
            send_sem=z_send.at[which, m], recv_sem=z_recv.at[slot, m],
            device_id={"chan": target}, device_id_type=MESH,
        )

    def got(slot, m):
        pltpu.make_async_copy(recv.at[slot, m], recv.at[slot, m], z_recv.at[slot, m]).wait()

    def when_in(step, lag, body):
        m = step - lag

        @pl.when(jnp.logical_and(m >= 0, m < bins))
        def _():
            body(m)

    @pl.when(is_mid)
    def _():
        has_1 = flags[0] == 1
        has_3 = flags[1] == 1

        def take_own(m):
            arrived(m)
            along(own, 1, m, 0, inner).start()
            flush(0, own, m).start()

        def take_outer(m):
            got(0, m)
            along(recv.at[0], 2, m, 1, inner).start()
            flush(1, recv.at[0], m).start()

        def take_inner(m):
            got(1, m)
            flush(2, recv.at[1], m).start()
            stage[0, m] = jnp.where(has_1, own[m], recv[1, m])
            along(stage.at[0], 0, m, 2, outer).start()

        def take_far(m):
            got(2, m)
            flush(3, recv.at[2], m).start()
            stage[1, m] = jnp.where(has_3, recv[2, m], recv[1, m])
            along(stage.at[1], 1, m, 3, outer).start()

        def step_mid(step, carry):
            when_in(step, 0, take_own)
            when_in(step, 1, take_outer)
            when_in(step, 1, take_inner)
            when_in(step, 2, take_far)
            return carry

        lax.fori_loop(0, bins + 2, step_mid, 0)

        def finish(m, carry):
            along(own, 1, m, 0, inner).wait_send()
            along(recv.at[0], 2, m, 1, inner).wait_send()
            along(stage.at[0], 0, m, 2, outer).wait_send()
            along(stage.at[1], 1, m, 3, outer).wait_send()
            flush(1, recv.at[0], m).wait()
            flush(2, recv.at[1], m).wait()
            flush(3, recv.at[2], m).wait()
            return carry

        lax.fori_loop(0, bins, finish, 0)

    @pl.when(is_end)
    def _():
        def take_own(m):
            arrived(m)
            along(own, 0, m, 0, next_in).start()
            flush(0, own, m).start()

        def take_first(m):
            got(0, m)
            flush(1, recv.at[0], m).start()

        def take_second(m):
            got(1, m)
            flush(2, recv.at[1], m).start()

        def step_end(step, carry):
            when_in(step, 0, take_own)
            when_in(step, 2, take_first)
            when_in(step, 2, take_second)
            return carry

        lax.fori_loop(0, bins + 2, step_end, 0)

        def finish(m, carry):
            along(own, 0, m, 0, next_in).wait_send()
            flush(1, recv.at[0], m).wait()
            flush(2, recv.at[1], m).wait()
            return carry

        lax.fori_loop(0, bins, finish, 0)

    def finish_all(m, carry):
        flush(0, own, m).wait()
        pltpu.make_async_copy(own.at[m, others], own.at[m, others], a2a_send.at[m]).wait()
        return carry

    lax.fori_loop(0, bins, finish_all, 0)


def exchange(x, flags):
    owners, bins, rows, channels = x.shape
    depth = owners * rows
    block = (bins, depth, channels)
    return pl.pallas_call(
        functools.partial(exchange_kernel, owners, bins, rows),
        out_shape=jax.ShapeDtypeStruct((4,) + block, x.dtype),
        in_specs=[pl.BlockSpec(memory_space=pltpu.SMEM), pl.BlockSpec(memory_space=pltpu.VMEM)],
        out_specs=pl.BlockSpec(memory_space=pl.ANY),
        scratch_shapes=[
            pltpu.VMEM(block, x.dtype),
            pltpu.VMEM((3,) + block, x.dtype),
            pltpu.VMEM((2,) + block, x.dtype),
            pltpu.SemaphoreType.DMA((bins,)),
            pltpu.SemaphoreType.DMA((bins,)),
            pltpu.SemaphoreType.DMA((4, bins)),
            pltpu.SemaphoreType.DMA((3, bins)),
            pltpu.SemaphoreType.DMA((4, bins)),
        ],
        compiler_params=pltpu.CompilerParams(
            collective_id=0, has_side_effects=True, vmem_limit_bytes=40 * 1024 * 1024
        ),
        name="exchange",
    )(flags, x)


def cross_kernel(scale, groups, rows, slots, own, first, second, out):
    half = rows // 2
    depth, channels = own.shape
    held = own[...].astype(jnp.float32).reshape(groups, rows, channels)
    turned = jnp.concatenate([held[:, half:], -held[:, :half]], axis=1)
    turned = turned.astype(jnp.bfloat16).reshape(depth, channels)
    for index, partner in enumerate((first, second)):
        for part, right in enumerate((own[...], turned)):
            product = lax.dot_general(
                partner[...], right, (((0,), (0,)), ((), ())), preferred_element_type=jnp.float32
            )
            out[index, part] = product * scale


def cross_terms(gathered, slots, groups, scale):
    _, bins, depth, channels = gathered.shape
    taken = lambda which: pl.BlockSpec(
        (None, None, depth, channels), lambda m, s: (s[which], m, 0, 0)
    )
    return pl.pallas_call(
        functools.partial(cross_kernel, scale, groups, depth // groups),
        out_shape=jax.ShapeDtypeStruct((bins, ROUNDS, 2, channels, channels), jnp.float32),
        grid_spec=pltpu.PrefetchScalarGridSpec(
            num_scalar_prefetch=1,
            grid=(bins,),
            in_specs=[
                pl.BlockSpec((None, None, depth, channels), lambda m, s: (0, m, 0, 0)),
                taken(0),
                taken(1),
            ],
            out_specs=pl.BlockSpec(
                (None, ROUNDS, 2, channels, channels), lambda m, s: (m, 0, 0, 0, 0)
            ),
        ),
        compiler_params=pltpu.CompilerParams(
            dimension_semantics=("arbitrary",), vmem_limit_bytes=40 * 1024 * 1024
        ),
        name="cross",
    )(slots, gathered, gathered, gathered)


def gather_images(x):
    owners, bins, rows, channels = x.shape
    swapped = lax.all_to_all(x, "win", 0, 0, tiled=True)
    images = [swapped.transpose(1, 0, 2, 3).reshape(bins, owners * rows, channels)]
    for bit_place in range(lax.axis_size("chan").bit_length() - 1):
        images = images + [from_partner(image, "chan", bit_place) for image in images]
    return jnp.stack(images)


def on_device(records, fir_taps, plan):
    channels, samples_here = records.shape
    window_count = samples_here // WL
    owners = lax.axis_size("win")
    chan = lax.axis_index("chan")
    scale = 1.0 / math.sqrt(window_count * owners)
    whitened = whiten(records, fir_taps)
    x = whitened.reshape(owners, F // owners, 2 * window_count, channels)
    keys = jnp.bitwise_xor(plan[:, chan], chan)
    if lax.axis_size("chan") == 4:
        has_1 = jnp.any(keys == 1)
        has_3 = jnp.any(keys == 3)
        flags = jnp.stack([has_1, has_3]).astype(jnp.int32)
        gathered = exchange(x, flags)
        at_mid = jnp.where(keys == 1, 1, jnp.where(keys == 3, 2, 3))
        at_end = jnp.where(keys == 1, 1, jnp.where(keys == 3, 2, jnp.where(has_1, 2, 1)))
        slots = jnp.where((chan == 1) | (chan == 2), at_mid, at_end)
    else:
        gathered = gather_images(x)
        slots = keys
    return cross_terms(gathered, slots.astype(jnp.int32), owners, scale)


def solution(mesh):
    placed = (P("chan", "win"), P(), P())
    return jax.shard_map(
        on_device,
        mesh=mesh,
        in_specs=placed,
        out_specs=P("win", None, None, None, "chan"),
        check_vma=False,
    )
```

```python
import functools
import math

import jax
import jax.numpy as jnp
import numpy as np
from jax import lax
from jax.experimental import pallas as pl
from jax.experimental.pallas import tpu as pltpu
from jax.sharding import PartitionSpec as P

WL = 256
F = 64
TAPS = 64
ROUNDS = 2
LEFT = 128
LEAD = 3
MESH = pl.DeviceIdType.MESH


def shifted(array, axis, by):
    count = lax.axis_size(axis)
    pairs = [(i, i + by) for i in range(count) if 0 <= i + by < count]
    return lax.ppermute(array, axis, pairs)


def from_partner(block, axis, bit):
    count = lax.axis_size(axis)
    route = []
    for low in range(count):
        high = low | 1 << bit
        if high != low and high < count:
            route += [(low, high), (high, low)]
    return lax.ppermute(block, axis, route)


def fir_matrix(fir_taps):
    inputs_at = jnp.arange(WL + TAPS - 1, dtype=jnp.int32)[:, None]
    outputs_at = jnp.arange(WL, dtype=jnp.int32)[None, :]
    tap_number = outputs_at + (TAPS - 1) - inputs_at
    inside = (tap_number >= 0) & (tap_number < TAPS)
    picked = fir_taps[jnp.clip(tap_number, 0, TAPS - 1)]
    return jnp.where(inside, picked, jnp.zeros_like(picked))


def dft_table():
    sample_at = jnp.arange(WL, dtype=jnp.int32)[:, None]
    column_at = jnp.arange(2 * F, dtype=jnp.int32)[None, :]
    bin_number = column_at // 2 + 1
    phases = (sample_at * bin_number % WL).astype(jnp.float32) * (2.0 * math.pi / WL)
    return jnp.where(column_at % 2 == 0, jnp.cos(phases), -jnp.sin(phases))


def split_table(fir_taps):
    table = jnp.dot(fir_matrix(fir_taps), dft_table(), precision=lax.Precision.HIGHEST)
    high = table.astype(jnp.bfloat16)
    low = (table - high.astype(jnp.float32)).astype(jnp.bfloat16)
    return jnp.concatenate([high, low], axis=1)


def whiten(records, fir_taps):
    channels, samples_here = records.shape
    window_count = samples_here // WL
    previous_tail = shifted(records[:, samples_here - TAPS + 1 :], "win", 1)
    samples = records.reshape(channels, window_count, WL)
    previous = jnp.concatenate(
        [previous_tail[:, None, :], samples[:, :-1, WL - TAPS + 1 :]], axis=1
    )
    table = split_table(fir_taps)
    both = jnp.einsum(
        "cwi,ik->kwc", samples, table[TAPS - 1 :], preferred_element_type=jnp.float32
    )
    both = both + jnp.einsum(
        "cwi,ik->kwc", previous, table[: TAPS - 1], preferred_element_type=jnp.float32
    )
    stacked = both[: 2 * F] + both[2 * F :]
    band_power = jnp.mean(stacked * stacked, axis=0, keepdims=True) + 1e-06
    return (stacked / jnp.sqrt(band_power)).astype(jnp.bfloat16)


def dft_rows(owners):
    bins = F // owners
    place = np.arange(bins)[:, None, None]
    owner = np.arange(owners)[None, :, None]
    part = np.arange(2)[None, None, :]
    number = np.broadcast_to(owner * bins + place + 1, (bins, owners, 2)).reshape(-1, 1)
    part = np.broadcast_to(part, (bins, owners, 2)).reshape(-1, 1)
    phases = (np.arange(WL)[None, :] * number % WL) * (2.0 * np.pi / WL)
    return np.where(part == 0, np.cos(phases), -np.sin(phases)).astype(np.float32)


def exchange_kernel(owners, bins, windows, plan, records, taps, dft, gathered,
                    table, halo, spectra, x, own, recv, stage,
                    halo_send, halo_recv, a2a_send, a2a_recv, z_send, z_recv, flush_sem):
    chan = lax.axis_index("chan")
    me = lax.axis_index("win")
    is_mid = jnp.logical_and(chan >= 1, chan <= 2)
    is_end = jnp.logical_not(is_mid)
    inner = 3 - chan
    outer = 3 * (chan - 1)
    next_in = 1 + chan // 3
    rows = 2 * windows
    kept = 2 * F
    lanes = spectra.shape[0]

    barrier = pltpu.get_barrier_semaphore()
    for step in range(1, owners):
        pl.semaphore_signal(barrier, inc=1, device_id={"win": lax.rem(me + step, owners)}, device_id_type=MESH)

    @pl.when(is_mid)
    def _():
        pl.semaphore_signal(barrier, inc=1, device_id={"chan": inner}, device_id_type=MESH)
        pl.semaphore_signal(barrier, inc=1, device_id={"chan": outer}, device_id_type=MESH)

    @pl.when(is_end)
    def _():
        pl.semaphore_signal(barrier, inc=1, device_id={"chan": next_in}, device_id_type=MESH)

    spread = jnp.broadcast_to(taps[...], (LEFT + WL, taps.shape[1]))
    shifted_taps = pltpu.roll(spread, 0, 1, stride=1, stride_axis=0)[:, LEFT : LEFT + WL]
    combined = lax.dot_general(
        dft[...], shifted_taps, (((1,), (1,)), ((), ())),
        precision=lax.Precision.HIGHEST, preferred_element_type=jnp.float32,
    )
    high = combined.astype(jnp.bfloat16)
    table[:kept] = high
    table[kept:] = (combined - high.astype(jnp.float32)).astype(jnp.bfloat16)

    pl.semaphore_wait(barrier, jnp.where(is_mid, owners + 1, owners))

    def tail_copy():
        return pltpu.make_async_remote_copy(
            src_ref=records.at[:, pl.ds(windows * WL - LEFT, LEFT)], dst_ref=halo,
            send_sem=halo_send, recv_sem=halo_recv,
            device_id={"win": lax.rem(me + 1, owners)}, device_id_type=MESH,
        )

    @pl.when(me < owners - 1)
    def _():
        tail_copy().start()

    def whiten_window(w, segment):
        both = lax.dot_general(
            table[...], segment, (((1,), (1,)), ((), ())), preferred_element_type=jnp.float32
        )
        stacked = both[:kept] + both[kept:]
        power = jnp.mean(stacked * stacked, axis=0, keepdims=True) + 1e-06
        whitened = stacked * (1.0 / jnp.sqrt(power))
        for lane in range(lanes):
            spectra[lane, pl.ds(pl.multiple_of(w * kept, kept), kept)] = whitened[
                :, lane * 128 : lane * 128 + 128
            ]

    def whiten_step(w, carry):
        start = pl.multiple_of(w * WL - LEFT, LEFT)
        whiten_window(w, records[:, pl.ds(start, LEFT + WL)])
        return carry

    lax.fori_loop(1, windows, whiten_step, 0)

    @pl.when(me == 0)
    def _():
        halo[...] = jnp.zeros_like(halo)

    @pl.when(me > 0)
    def _():
        pltpu.make_async_copy(halo, halo, halo_recv).wait()

    whiten_window(0, jnp.concatenate([halo[...], records[:, :WL]], axis=1))

    mine = pl.ds(pl.multiple_of(me * rows, rows), rows)

    def start_block(m):
        for owner in range(owners):
            first = (m * owners + owner) * 2
            for lane in range(lanes):
                real = spectra[lane, pl.ds(first, windows, stride=kept)]
                imag = spectra[lane, pl.ds(first + 1, windows, stride=kept)]
                x[m, owner, :, lane * 128 : lane * 128 + 128] = jnp.concatenate(
                    [real, imag], axis=0
                ).astype(jnp.bfloat16)
        for step in range(1, owners):
            target = lax.rem(me + step, owners)
            pltpu.make_async_remote_copy(
                src_ref=x.at[m, target], dst_ref=own.at[m, mine],
                send_sem=a2a_send.at[m], recv_sem=a2a_recv.at[m],
                device_id={"win": target}, device_id_type=MESH,
            ).start()
        own[m, mine] = x[m, me]

    others = pl.ds(0, (owners - 1) * rows)

    def arrived(m):
        pltpu.make_async_copy(own.at[m, others], own.at[m, others], a2a_recv.at[m]).wait()

    def flush(slot, source, m):
        return pltpu.make_async_copy(source.at[m], gathered.at[slot, m], flush_sem.at[slot, m])

    def along(source, slot, m, which, target):
        return pltpu.make_async_remote_copy(
            src_ref=source.at[m], dst_ref=recv.at[slot, m],
            send_sem=z_send.at[which, m], recv_sem=z_recv.at[slot, m],
            device_id={"chan": target}, device_id_type=MESH,
        )

    def got(slot, m):
        pltpu.make_async_copy(recv.at[slot, m], recv.at[slot, m], z_recv.at[slot, m]).wait()

    def when_in(step, lag, body):
        m = step - lag

        @pl.when(jnp.logical_and(m >= 0, m < bins))
        def _():
            body(m)

    @pl.when(is_mid)
    def _():
        has_1 = jnp.logical_or(plan[0, 0] == 1, plan[1, 0] == 1)
        has_3 = jnp.logical_or(plan[0, 0] == 3, plan[1, 0] == 3)

        def take_own(m):
            arrived(m)
            along(own, 1, m, 0, inner).start()
            flush(0, own, m).start()

        def take_outer(m):
            got(0, m)
            along(recv.at[0], 2, m, 1, inner).start()
            flush(1, recv.at[0], m).start()

        def take_inner(m):
            got(1, m)
            flush(2, recv.at[1], m).start()
            stage[0, m] = jnp.where(has_1, own[m], recv[1, m])
            along(stage.at[0], 0, m, 2, outer).start()

        def take_far(m):
            got(2, m)
            flush(3, recv.at[2], m).start()
            stage[1, m] = jnp.where(has_3, recv[2, m], recv[1, m])
            along(stage.at[1], 1, m, 3, outer).start()

        def step_mid(step, carry):
            when_in(step, 0, start_block)
            when_in(step, LEAD, take_own)
            when_in(step, LEAD + 1, take_outer)
            when_in(step, LEAD + 1, take_inner)
            when_in(step, LEAD + 2, take_far)
            return carry

        lax.fori_loop(0, bins + LEAD + 2, step_mid, 0)

        def finish(m, carry):
            along(own, 1, m, 0, inner).wait_send()
            along(recv.at[0], 2, m, 1, inner).wait_send()
            along(stage.at[0], 0, m, 2, outer).wait_send()
            along(stage.at[1], 1, m, 3, outer).wait_send()
            flush(1, recv.at[0], m).wait()
            flush(2, recv.at[1], m).wait()
            flush(3, recv.at[2], m).wait()
            return carry

        lax.fori_loop(0, bins, finish, 0)

    @pl.when(is_end)
    def _():
        def take_own(m):
            arrived(m)
            along(own, 0, m, 0, next_in).start()
            flush(0, own, m).start()

        def take_first(m):
            got(0, m)
            flush(1, recv.at[0], m).start()

        def take_second(m):
            got(1, m)
            flush(2, recv.at[1], m).start()

        def step_end(step, carry):
            when_in(step, 0, start_block)
            when_in(step, LEAD, take_own)
            when_in(step, LEAD + 2, take_first)
            when_in(step, LEAD + 2, take_second)
            return carry

        lax.fori_loop(0, bins + LEAD + 2, step_end, 0)

        def finish(m, carry):
            along(own, 0, m, 0, next_in).wait_send()
            flush(1, recv.at[0], m).wait()
            flush(2, recv.at[1], m).wait()
            return carry

        lax.fori_loop(0, bins, finish, 0)

    def finish_all(m, carry):
        flush(0, own, m).wait()
        pltpu.make_async_copy(own.at[m, others], own.at[m, others], a2a_send.at[m]).wait()
        return carry

    lax.fori_loop(0, bins, finish_all, 0)

    @pl.when(me < owners - 1)
    def _():
        tail_copy().wait_send()


def exchange(records, fir_taps, plan):
    channels, samples_here = records.shape
    owners = lax.axis_size("win")
    bins, windows = F // owners, samples_here // WL
    block = (bins, owners * 2 * windows, channels)
    taps = jnp.pad(fir_taps[None, :], ((0, 0), (0, LEFT + WL + LEFT - TAPS)))
    in_vmem = pl.BlockSpec(memory_space=pltpu.VMEM)
    return pl.pallas_call(
        functools.partial(exchange_kernel, owners, bins, windows),
        out_shape=jax.ShapeDtypeStruct((4,) + block, jnp.bfloat16),
        in_specs=[pl.BlockSpec(memory_space=pltpu.SMEM), in_vmem, in_vmem, in_vmem],
        out_specs=pl.BlockSpec(memory_space=pl.ANY),
        scratch_shapes=[
            pltpu.VMEM((4 * F, LEFT + WL), jnp.bfloat16),
            pltpu.VMEM((channels, LEFT), jnp.bfloat16),
            pltpu.VMEM((channels // 128, windows * 2 * F, 128), jnp.float32),
            pltpu.VMEM((bins, owners, 2 * windows, channels), jnp.bfloat16),
            pltpu.VMEM(block, jnp.bfloat16),
            pltpu.VMEM((3,) + block, jnp.bfloat16),
            pltpu.VMEM((2,) + block, jnp.bfloat16),
            pltpu.SemaphoreType.DMA,
            pltpu.SemaphoreType.DMA,
            pltpu.SemaphoreType.DMA((bins,)),
            pltpu.SemaphoreType.DMA((bins,)),
            pltpu.SemaphoreType.DMA((4, bins)),
            pltpu.SemaphoreType.DMA((3, bins)),
            pltpu.SemaphoreType.DMA((4, bins)),
        ],
        compiler_params=pltpu.CompilerParams(
            collective_id=0, has_side_effects=True, vmem_limit_bytes=52 * 1024 * 1024
        ),
        name="exchange",
    )(plan, records, taps, jnp.asarray(dft_rows(owners)))


def cross_kernel(scale, groups, rows, slots, own, first, second, out):
    half = rows // 2
    depth, channels = own.shape
    held = own[...].astype(jnp.float32).reshape(groups, rows, channels)
    turned = jnp.concatenate([held[:, half:], -held[:, :half]], axis=1)
    turned = turned.astype(jnp.bfloat16).reshape(depth, channels)
    for index, partner in enumerate((first, second)):
        for part, right in enumerate((own[...], turned)):
            product = lax.dot_general(
                partner[...], right, (((0,), (0,)), ((), ())), preferred_element_type=jnp.float32
            )
            out[index, part] = product * scale


def cross_terms(gathered, slots, groups, scale):
    _, bins, depth, channels = gathered.shape
    taken = lambda which: pl.BlockSpec(
        (None, None, depth, channels), lambda m, s: (s[which], m, 0, 0)
    )
    return pl.pallas_call(
        functools.partial(cross_kernel, scale, groups, depth // groups),
        out_shape=jax.ShapeDtypeStruct((bins, ROUNDS, 2, channels, channels), jnp.float32),
        grid_spec=pltpu.PrefetchScalarGridSpec(
            num_scalar_prefetch=1,
            grid=(bins,),
            in_specs=[
                pl.BlockSpec((None, None, depth, channels), lambda m, s: (0, m, 0, 0)),
                taken(0),
                taken(1),
            ],
            out_specs=pl.BlockSpec(
                (None, ROUNDS, 2, channels, channels), lambda m, s: (m, 0, 0, 0, 0)
            ),
        ),
        compiler_params=pltpu.CompilerParams(
            dimension_semantics=("arbitrary",), vmem_limit_bytes=40 * 1024 * 1024
        ),
        name="cross",
    )(slots, gathered, gathered, gathered)


def gather_images(x):
    owners, bins, rows, channels = x.shape
    swapped = lax.all_to_all(x, "win", 0, 0, tiled=True)
    images = [swapped.transpose(1, 0, 2, 3).reshape(bins, owners * rows, channels)]
    for bit_place in range(lax.axis_size("chan").bit_length() - 1):
        images = images + [from_partner(image, "chan", bit_place) for image in images]
    return jnp.stack(images)


def on_device(records, fir_taps, plan):
    channels, samples_here = records.shape
    window_count = samples_here // WL
    owners = lax.axis_size("win")
    chan = lax.axis_index("chan")
    scale = 1.0 / math.sqrt(window_count * owners)
    keys = jnp.bitwise_xor(plan[:, chan], chan)
    if lax.axis_size("chan") == 4:
        has_1 = jnp.any(keys == 1)
        gathered = exchange(records, fir_taps, plan)
        at_mid = jnp.where(keys == 1, 1, jnp.where(keys == 3, 2, 3))
        at_end = jnp.where(keys == 1, 1, jnp.where(keys == 3, 2, jnp.where(has_1, 2, 1)))
        slots = jnp.where((chan == 1) | (chan == 2), at_mid, at_end)
    else:
        whitened = whiten(records, fir_taps)
        gathered = gather_images(
            whitened.reshape(owners, F // owners, 2 * window_count, channels)
        )
        slots = keys
    return cross_terms(gathered, slots.astype(jnp.int32), owners, scale)


def solution(mesh):
    placed = (P("chan", "win"), P(), P())
    return jax.shard_map(
        on_device,
        mesh=mesh,
        in_specs=placed,
        out_specs=P("win", None, None, None, "chan"),
        check_vma=False,
    )
```

```python
import functools
import math

import jax
import jax.numpy as jnp
import numpy as np
from jax import lax
from jax.experimental import pallas as pl
from jax.experimental.pallas import tpu as pltpu
from jax.sharding import PartitionSpec as P

WL = 256
F = 64
TAPS = 64
ROUNDS = 2
LEFT = 128
GROUP = 8
PER_CHUNK = 2
LEAD = 4
MESH = pl.DeviceIdType.MESH


def shifted(array, axis, by):
    count = lax.axis_size(axis)
    pairs = [(i, i + by) for i in range(count) if 0 <= i + by < count]
    return lax.ppermute(array, axis, pairs)


def from_partner(block, axis, bit):
    count = lax.axis_size(axis)
    route = []
    for low in range(count):
        high = low | 1 << bit
        if high != low and high < count:
            route += [(low, high), (high, low)]
    return lax.ppermute(block, axis, route)


def fir_matrix(fir_taps):
    inputs_at = jnp.arange(WL + TAPS - 1, dtype=jnp.int32)[:, None]
    outputs_at = jnp.arange(WL, dtype=jnp.int32)[None, :]
    tap_number = outputs_at + (TAPS - 1) - inputs_at
    inside = (tap_number >= 0) & (tap_number < TAPS)
    picked = fir_taps[jnp.clip(tap_number, 0, TAPS - 1)]
    return jnp.where(inside, picked, jnp.zeros_like(picked))


def dft_table():
    sample_at = jnp.arange(WL, dtype=jnp.int32)[:, None]
    column_at = jnp.arange(2 * F, dtype=jnp.int32)[None, :]
    bin_number = column_at // 2 + 1
    phases = (sample_at * bin_number % WL).astype(jnp.float32) * (2.0 * math.pi / WL)
    return jnp.where(column_at % 2 == 0, jnp.cos(phases), -jnp.sin(phases))


def split_table(fir_taps):
    table = jnp.dot(fir_matrix(fir_taps), dft_table(), precision=lax.Precision.HIGHEST)
    high = table.astype(jnp.bfloat16)
    low = (table - high.astype(jnp.float32)).astype(jnp.bfloat16)
    return jnp.concatenate([high, low], axis=1)


def whiten(records, fir_taps):
    channels, samples_here = records.shape
    window_count = samples_here // WL
    previous_tail = shifted(records[:, samples_here - TAPS + 1 :], "win", 1)
    samples = records.reshape(channels, window_count, WL)
    previous = jnp.concatenate(
        [previous_tail[:, None, :], samples[:, :-1, WL - TAPS + 1 :]], axis=1
    )
    table = split_table(fir_taps)
    both = jnp.einsum(
        "cwi,ik->kwc", samples, table[TAPS - 1 :], preferred_element_type=jnp.float32
    )
    both = both + jnp.einsum(
        "cwi,ik->kwc", previous, table[: TAPS - 1], preferred_element_type=jnp.float32
    )
    stacked = both[: 2 * F] + both[2 * F :]
    band_power = jnp.mean(stacked * stacked, axis=0, keepdims=True) + 1e-06
    return (stacked / jnp.sqrt(band_power)).astype(jnp.bfloat16)


def dft_rows(owners):
    bins = F // owners
    place = np.arange(bins)[:, None, None]
    owner = np.arange(owners)[None, :, None]
    part = np.arange(2)[None, None, :]
    number = np.broadcast_to(owner * bins + place + 1, (bins, owners, 2)).reshape(-1, 1)
    part = np.broadcast_to(part, (bins, owners, 2)).reshape(-1, 1)
    phases = (np.arange(WL)[None, :] * number % WL) * (2.0 * np.pi / WL)
    return np.where(part == 0, np.cos(phases), -np.sin(phases)).astype(np.float32)


def exchange_kernel(owners, bins, windows, scale, plan, records, taps, dft, out,
                    rec, table, halo, spectra, x, own, recv, stage, acc, result,
                    rec_sem, halo_send, halo_recv, a2a_send, a2a_recv, z_send, z_recv, out_sem):
    chan = lax.axis_index("chan")
    me = lax.axis_index("win")
    is_mid = jnp.logical_and(chan >= 1, chan <= 2)
    is_end = jnp.logical_not(is_mid)
    inner = 3 - chan
    outer = 3 * (chan - 1)
    next_in = 1 + chan // 3
    kept = 2 * F
    lanes = spectra.shape[0]
    groups = windows // GROUP
    pairs = bins // PER_CHUNK
    chunks = groups * pairs
    span = GROUP * WL
    unit = 2 * GROUP

    def load(g):
        columns = pl.ds(pl.multiple_of(g * span, span), span)
        return pltpu.make_async_copy(records.at[:, columns], rec.at[:, columns], rec_sem.at[g])

    for g in range(groups):
        load(g).start()

    barrier = pltpu.get_barrier_semaphore()
    for step in range(1, owners):
        pl.semaphore_signal(barrier, inc=1, device_id={"win": lax.rem(me + step, owners)}, device_id_type=MESH)

    @pl.when(is_mid)
    def _():
        pl.semaphore_signal(barrier, inc=1, device_id={"chan": inner}, device_id_type=MESH)
        pl.semaphore_signal(barrier, inc=1, device_id={"chan": outer}, device_id_type=MESH)

    @pl.when(is_end)
    def _():
        pl.semaphore_signal(barrier, inc=1, device_id={"chan": next_in}, device_id_type=MESH)

    spread = jnp.broadcast_to(taps[...], (LEFT + WL, taps.shape[1]))
    shifted_taps = pltpu.roll(spread, 0, 1, stride=1, stride_axis=0)[:, LEFT : LEFT + WL]
    combined = lax.dot_general(
        dft[...], shifted_taps, (((1,), (1,)), ((), ())),
        precision=lax.Precision.HIGHEST, preferred_element_type=jnp.float32,
    )
    high = combined.astype(jnp.bfloat16)
    table[:kept] = high
    table[kept:] = (combined - high.astype(jnp.float32)).astype(jnp.bfloat16)

    pl.semaphore_wait(barrier, jnp.where(is_mid, owners + 1, owners))

    def tail_copy():
        return pltpu.make_async_remote_copy(
            src_ref=records.at[:, pl.ds(windows * WL - LEFT, LEFT)], dst_ref=halo,
            send_sem=halo_send, recv_sem=halo_recv,
            device_id={"win": lax.rem(me + 1, owners)}, device_id_type=MESH,
        )

    @pl.when(me < owners - 1)
    def _():
        tail_copy().start()

    def whiten_window(place, segment):
        both = lax.dot_general(
            table[...], segment, (((1,), (1,)), ((), ())), preferred_element_type=jnp.float32
        )
        stacked = both[:kept] + both[kept:]
        power = jnp.mean(stacked * stacked, axis=0, keepdims=True) + 1e-06
        whitened = stacked * (1.0 / jnp.sqrt(power))
        for lane in range(lanes):
            spectra[lane, pl.ds(place * kept, kept)] = whitened[:, lane * 128 : lane * 128 + 128]

    def whiten_group(turn):
        g = lax.rem(turn + 1, groups)
        base = g * span

        @pl.when(turn == 0)
        def _():
            load(0).wait()

        @pl.when(g > 0)
        def _():
            load(g).wait()
            whiten_window(0, rec[:, pl.ds(pl.multiple_of(base - LEFT, LEFT), LEFT + WL)])

        @pl.when(jnp.logical_and(g == 0, me == 0))
        def _():
            halo[...] = jnp.zeros_like(halo)

        @pl.when(jnp.logical_and(g == 0, me > 0))
        def _():
            pltpu.make_async_copy(halo, halo, halo_recv).wait()

        @pl.when(g == 0)
        def _():
            whiten_window(0, jnp.concatenate([halo[...], rec[:, :WL]], axis=1))

        for place in range(1, GROUP):
            start = pl.multiple_of(base + place * WL - LEFT, LEFT)
            whiten_window(place, rec[:, pl.ds(start, LEFT + WL)])

    mine = pl.ds(pl.multiple_of(me * unit, unit), unit)

    def start_block(n):
        pair = lax.rem(n, pairs)

        @pl.when(pair == 0)
        def _():
            whiten_group(n // pairs)

        for b in range(PER_CHUNK):
            for owner in range(owners):
                first = ((pair * PER_CHUNK + b) * owners + owner) * 2
                for lane in range(lanes):
                    real = spectra[lane, pl.ds(first, GROUP, stride=kept)]
                    imag = spectra[lane, pl.ds(first + 1, GROUP, stride=kept)]
                    x[n, owner, b, :, lane * 128 : lane * 128 + 128] = jnp.concatenate(
                        [real, imag], axis=0
                    ).astype(jnp.bfloat16)
        for step in range(1, owners):
            target = lax.rem(me + step, owners)
            pltpu.make_async_remote_copy(
                src_ref=x.at[n, target], dst_ref=own.at[n, :, mine],
                send_sem=a2a_send.at[n], recv_sem=a2a_recv.at[n],
                device_id={"win": target}, device_id_type=MESH,
            ).start()
        own[n, :, mine] = x[n, me]

    others = pl.ds(0, (owners - 1) * unit)

    def arrived(n):
        pltpu.make_async_copy(own.at[n, :, others], own.at[n, :, others], a2a_recv.at[n]).wait()

    def along(source, slot, n, which, target):
        return pltpu.make_async_remote_copy(
            src_ref=source.at[n], dst_ref=recv.at[slot, n],
            send_sem=z_send.at[which, n], recv_sem=z_recv.at[slot, n],
            device_id={"chan": target}, device_id_type=MESH,
        )

    def got(slot, n):
        pltpu.make_async_copy(recv.at[slot, n], recv.at[slot, n], z_recv.at[slot, n]).wait()

    def flush(pair):
        place = pl.ds(pair * PER_CHUNK, PER_CHUNK)
        return pltpu.make_async_copy(result.at[place], out.at[place], out_sem.at[pair])

    def multiply(n, choose):
        pair = lax.rem(n, pairs)
        started = n >= pairs
        for b in range(PER_CHUNK):
            at = pair * PER_CHUNK + b
            mine_now = own[n, b]
            depth, channels = mine_now.shape
            held = mine_now.astype(jnp.float32).reshape(owners, unit, channels)
            turned = jnp.concatenate([held[:, GROUP:], -held[:, :GROUP]], axis=1)
            turned = turned.astype(jnp.bfloat16).reshape(depth, channels)
            right = jnp.concatenate([mine_now, turned], axis=1)
            for index in range(ROUNDS):
                product = lax.dot_general(
                    choose(index, b), right, (((0,), (0,)), ((), ())),
                    preferred_element_type=jnp.float32,
                )
                acc[at, index] = jnp.where(started, acc[at, index], 0.0) + product

        @pl.when(n >= chunks - pairs)
        def _():
            for b in range(PER_CHUNK):
                at = pair * PER_CHUNK + b
                for index in range(ROUNDS):
                    total = (acc[at, index] * scale).astype(result.dtype)
                    for part in range(2):
                        result[at, index, part] = total[:, part * channels : (part + 1) * channels]
            flush(pair).start()

    def when_in(step, lag, body):
        n = step - lag

        @pl.when(jnp.logical_and(n >= 0, n < chunks))
        def _():
            body(n)

    keys = [plan[index, 0] for index in range(ROUNDS)]
    has_1 = jnp.logical_or(keys[0] == 1, keys[1] == 1)
    has_3 = jnp.logical_or(keys[0] == 3, keys[1] == 3)

    @pl.when(is_mid)
    def _():
        def take_own(n):
            arrived(n)
            along(own, 1, n, 0, inner).start()

        def take_outer(n):
            got(0, n)
            along(recv.at[0], 2, n, 1, inner).start()

        def take_inner(n):
            got(1, n)
            stage[0, n] = jnp.where(has_1, own[n], recv[1, n])
            along(stage.at[0], 0, n, 2, outer).start()

        def take_far(n):
            got(2, n)
            stage[1, n] = jnp.where(has_3, recv[2, n], recv[1, n])
            along(stage.at[1], 1, n, 3, outer).start()

            def choose(index, b):
                key = keys[index]
                later = jnp.where(key == 3, recv[1, n, b], recv[2, n, b])
                return jnp.where(key == 1, recv[0, n, b], later)

            multiply(n, choose)

        def step_mid(step, carry):
            when_in(step, 0, start_block)
            when_in(step, LEAD, take_own)
            when_in(step, LEAD + 1, take_outer)
            when_in(step, LEAD + 2, take_inner)
            when_in(step, LEAD + 3, take_far)
            return carry

        lax.fori_loop(0, chunks + LEAD + 3, step_mid, 0)

        def finish(n, carry):
            along(own, 1, n, 0, inner).wait_send()
            along(recv.at[0], 2, n, 1, inner).wait_send()
            along(stage.at[0], 0, n, 2, outer).wait_send()
            along(stage.at[1], 1, n, 3, outer).wait_send()
            return carry

        lax.fori_loop(0, chunks, finish, 0)

    @pl.when(is_end)
    def _():
        def take_own(n):
            arrived(n)
            along(own, 0, n, 0, next_in).start()

        def take_both(n):
            got(0, n)
            got(1, n)

            def choose(index, b):
                key = keys[index]
                in_first = jnp.logical_or(
                    key == 1, jnp.logical_and(key == 2, jnp.logical_not(has_1))
                )
                return jnp.where(in_first, recv[0, n, b], recv[1, n, b])

            multiply(n, choose)

        def step_end(step, carry):
            when_in(step, 0, start_block)
            when_in(step, LEAD, take_own)
            when_in(step, LEAD + 5, take_both)
            return carry

        lax.fori_loop(0, chunks + LEAD + 5, step_end, 0)

        def finish(n, carry):
            along(own, 0, n, 0, next_in).wait_send()
            return carry

        lax.fori_loop(0, chunks, finish, 0)

    def finish_all(n, carry):
        pltpu.make_async_copy(own.at[n, :, others], own.at[n, :, others], a2a_send.at[n]).wait()
        return carry

    lax.fori_loop(0, chunks, finish_all, 0)
    for pair in range(pairs):
        flush(pair).wait()

    @pl.when(me < owners - 1)
    def _():
        tail_copy().wait_send()


def exchange(records, fir_taps, plan, scale):
    channels, samples_here = records.shape
    owners = lax.axis_size("win")
    bins, windows = F // owners, samples_here // WL
    chunks = (windows // GROUP) * (bins // PER_CHUNK)
    block = (chunks, PER_CHUNK, owners * 2 * GROUP, channels)
    taps = jnp.pad(fir_taps[None, :], ((0, 0), (0, LEFT + WL + LEFT - TAPS)))
    in_vmem = pl.BlockSpec(memory_space=pltpu.VMEM)
    in_place = pl.BlockSpec(memory_space=pl.ANY)
    result = (bins, ROUNDS, 2, channels, channels)
    return pl.pallas_call(
        functools.partial(exchange_kernel, owners, bins, windows, scale),
        out_shape=jax.ShapeDtypeStruct(result, jnp.bfloat16),
        in_specs=[pl.BlockSpec(memory_space=pltpu.SMEM), in_place, in_vmem, in_vmem],
        out_specs=in_place,
        scratch_shapes=[
            pltpu.VMEM(records.shape, jnp.bfloat16),
            pltpu.VMEM((4 * F, LEFT + WL), jnp.bfloat16),
            pltpu.VMEM((channels, LEFT), jnp.bfloat16),
            pltpu.VMEM((channels // 128, GROUP * 2 * F, 128), jnp.float32),
            pltpu.VMEM((chunks, owners, PER_CHUNK, 2 * GROUP, channels), jnp.bfloat16),
            pltpu.VMEM(block, jnp.bfloat16),
            pltpu.VMEM((3,) + block, jnp.bfloat16),
            pltpu.VMEM((2,) + block, jnp.bfloat16),
            pltpu.VMEM((bins, ROUNDS, channels, 2 * channels), jnp.float32),
            pltpu.VMEM(result, jnp.bfloat16),
            pltpu.SemaphoreType.DMA((windows // GROUP,)),
            pltpu.SemaphoreType.DMA,
            pltpu.SemaphoreType.DMA,
            pltpu.SemaphoreType.DMA((chunks,)),
            pltpu.SemaphoreType.DMA((chunks,)),
            pltpu.SemaphoreType.DMA((4, chunks)),
            pltpu.SemaphoreType.DMA((3, chunks)),
            pltpu.SemaphoreType.DMA((bins // PER_CHUNK,)),
        ],
        compiler_params=pltpu.CompilerParams(
            collective_id=0, has_side_effects=True, vmem_limit_bytes=48 * 1024 * 1024
        ),
        name="exchange",
    )(plan, records, taps, jnp.asarray(dft_rows(owners)))


def cross_kernel(scale, groups, rows, slots, own, first, second, out):
    half = rows // 2
    depth, channels = own.shape
    held = own[...].astype(jnp.float32).reshape(groups, rows, channels)
    turned = jnp.concatenate([held[:, half:], -held[:, :half]], axis=1)
    turned = turned.astype(jnp.bfloat16).reshape(depth, channels)
    for index, partner in enumerate((first, second)):
        for part, right in enumerate((own[...], turned)):
            product = lax.dot_general(
                partner[...], right, (((0,), (0,)), ((), ())), preferred_element_type=jnp.float32
            )
            out[index, part] = product * scale


def cross_terms(gathered, slots, groups, scale):
    _, bins, depth, channels = gathered.shape
    taken = lambda which: pl.BlockSpec(
        (None, None, depth, channels), lambda m, s: (s[which], m, 0, 0)
    )
    return pl.pallas_call(
        functools.partial(cross_kernel, scale, groups, depth // groups),
        out_shape=jax.ShapeDtypeStruct((bins, ROUNDS, 2, channels, channels), jnp.float32),
        grid_spec=pltpu.PrefetchScalarGridSpec(
            num_scalar_prefetch=1,
            grid=(bins,),
            in_specs=[
                pl.BlockSpec((None, None, depth, channels), lambda m, s: (0, m, 0, 0)),
                taken(0),
                taken(1),
            ],
            out_specs=pl.BlockSpec(
                (None, ROUNDS, 2, channels, channels), lambda m, s: (m, 0, 0, 0, 0)
            ),
        ),
        compiler_params=pltpu.CompilerParams(
            dimension_semantics=("arbitrary",), vmem_limit_bytes=40 * 1024 * 1024
        ),
        name="cross",
    )(slots, gathered, gathered, gathered)


def gather_images(x):
    owners, bins, rows, channels = x.shape
    swapped = lax.all_to_all(x, "win", 0, 0, tiled=True)
    images = [swapped.transpose(1, 0, 2, 3).reshape(bins, owners * rows, channels)]
    for bit_place in range(lax.axis_size("chan").bit_length() - 1):
        images = images + [from_partner(image, "chan", bit_place) for image in images]
    return jnp.stack(images)


def on_device(records, fir_taps, plan):
    channels, samples_here = records.shape
    window_count = samples_here // WL
    owners = lax.axis_size("win")
    chan = lax.axis_index("chan")
    scale = 1.0 / math.sqrt(window_count * owners)
    keys = jnp.bitwise_xor(plan[:, chan], chan)
    if lax.axis_size("chan") == 4:
        return exchange(records, fir_taps, plan, scale).astype(jnp.float32)
    whitened = whiten(records, fir_taps)
    gathered = gather_images(
        whitened.reshape(owners, F // owners, 2 * window_count, channels)
    )
    return cross_terms(gathered, keys.astype(jnp.int32), owners, scale)


def solution(mesh):
    placed = (P("chan", "win"), P(), P())
    return jax.shard_map(
        on_device,
        mesh=mesh,
        in_specs=placed,
        out_specs=P("win", None, None, None, "chan"),
        check_vma=False,
    )
```

```python
import functools
import math

import jax
import jax.numpy as jnp
import numpy as np
from jax import lax
from jax.experimental import pallas as pl
from jax.experimental.pallas import tpu as pltpu
from jax.sharding import PartitionSpec as P

WL = 256
F = 64
TAPS = 64
ROUNDS = 2
LEFT = 128
GROUP = 8
PER_CHUNK = 1
LEAD = 4
MESH = pl.DeviceIdType.MESH


def shifted(array, axis, by):
    count = lax.axis_size(axis)
    pairs = [(i, i + by) for i in range(count) if 0 <= i + by < count]
    return lax.ppermute(array, axis, pairs)


def from_partner(block, axis, bit):
    count = lax.axis_size(axis)
    route = []
    for low in range(count):
        high = low | 1 << bit
        if high != low and high < count:
            route += [(low, high), (high, low)]
    return lax.ppermute(block, axis, route)


def fir_matrix(fir_taps):
    inputs_at = jnp.arange(WL + TAPS - 1, dtype=jnp.int32)[:, None]
    outputs_at = jnp.arange(WL, dtype=jnp.int32)[None, :]
    tap_number = outputs_at + (TAPS - 1) - inputs_at
    inside = (tap_number >= 0) & (tap_number < TAPS)
    picked = fir_taps[jnp.clip(tap_number, 0, TAPS - 1)]
    return jnp.where(inside, picked, jnp.zeros_like(picked))


def dft_table():
    sample_at = jnp.arange(WL, dtype=jnp.int32)[:, None]
    column_at = jnp.arange(2 * F, dtype=jnp.int32)[None, :]
    bin_number = column_at // 2 + 1
    phases = (sample_at * bin_number % WL).astype(jnp.float32) * (2.0 * math.pi / WL)
    return jnp.where(column_at % 2 == 0, jnp.cos(phases), -jnp.sin(phases))


def split_table(fir_taps):
    table = jnp.dot(fir_matrix(fir_taps), dft_table(), precision=lax.Precision.HIGHEST)
    high = table.astype(jnp.bfloat16)
    low = (table - high.astype(jnp.float32)).astype(jnp.bfloat16)
    return jnp.concatenate([high, low], axis=1)


def whiten(records, fir_taps):
    channels, samples_here = records.shape
    window_count = samples_here // WL
    previous_tail = shifted(records[:, samples_here - TAPS + 1 :], "win", 1)
    samples = records.reshape(channels, window_count, WL)
    previous = jnp.concatenate(
        [previous_tail[:, None, :], samples[:, :-1, WL - TAPS + 1 :]], axis=1
    )
    table = split_table(fir_taps)
    both = jnp.einsum(
        "cwi,ik->kwc", samples, table[TAPS - 1 :], preferred_element_type=jnp.float32
    )
    both = both + jnp.einsum(
        "cwi,ik->kwc", previous, table[: TAPS - 1], preferred_element_type=jnp.float32
    )
    stacked = both[: 2 * F] + both[2 * F :]
    band_power = jnp.mean(stacked * stacked, axis=0, keepdims=True) + 1e-06
    return (stacked / jnp.sqrt(band_power)).astype(jnp.bfloat16)


def dft_rows(owners):
    bins = F // owners
    place = np.arange(bins)[:, None, None]
    owner = np.arange(owners)[None, :, None]
    part = np.arange(2)[None, None, :]
    number = np.broadcast_to(owner * bins + place + 1, (bins, owners, 2)).reshape(-1, 1)
    part = np.broadcast_to(part, (bins, owners, 2)).reshape(-1, 1)
    phases = (np.arange(WL)[None, :] * number % WL) * (2.0 * np.pi / WL)
    return np.where(part == 0, np.cos(phases), -np.sin(phases)).astype(np.float32)


def exchange_kernel(owners, bins, windows, scale, plan_at, records, taps_at, dft_at, out,
                    plan, taps, dft, rec, table, halo, spectra, x, own, recv, stage, acc, result,
                    small_sem, rec_sem, halo_send, halo_recv, a2a_send, a2a_recv, z_send, z_recv, out_sem):
    chan = lax.axis_index("chan")
    me = lax.axis_index("win")
    is_mid = jnp.logical_and(chan >= 1, chan <= 2)
    is_end = jnp.logical_not(is_mid)
    inner = 3 - chan
    outer = 3 * (chan - 1)
    next_in = 1 + chan // 3
    kept = 2 * F
    lanes = spectra.shape[0]
    groups = windows // GROUP
    pairs = bins // PER_CHUNK
    chunks = groups * pairs
    span = GROUP * WL
    unit = 2 * GROUP

    def load(g):
        columns = pl.ds(pl.multiple_of(g * span, span), span)
        return pltpu.make_async_copy(records.at[:, columns], rec.at[:, columns], rec_sem.at[g])

    small = [
        pltpu.make_async_copy(source, target, small_sem.at[place])
        for place, (source, target) in enumerate(((taps_at, taps), (dft_at, dft), (plan_at, plan)))
    ]
    for copy in small:
        copy.start()
    for g in range(groups):
        load(g).start()

    barrier = pltpu.get_barrier_semaphore()
    for step in range(1, owners):
        pl.semaphore_signal(barrier, inc=1, device_id={"win": lax.rem(me + step, owners)}, device_id_type=MESH)

    @pl.when(is_mid)
    def _():
        pl.semaphore_signal(barrier, inc=1, device_id={"chan": inner}, device_id_type=MESH)
        pl.semaphore_signal(barrier, inc=1, device_id={"chan": outer}, device_id_type=MESH)

    @pl.when(is_end)
    def _():
        pl.semaphore_signal(barrier, inc=1, device_id={"chan": next_in}, device_id_type=MESH)

    for copy in small:
        copy.wait()
    row = jnp.concatenate([taps[...], jnp.zeros((1, LEFT + WL + LEFT - TAPS), jnp.float32)], axis=1)
    spread = jnp.broadcast_to(row, (LEFT + WL, LEFT + WL + LEFT))
    shifted_taps = pltpu.roll(spread, 0, 1, stride=1, stride_axis=0)[:, LEFT : LEFT + WL]
    combined = lax.dot_general(
        dft[...], shifted_taps, (((1,), (1,)), ((), ())),
        precision=lax.Precision.HIGHEST, preferred_element_type=jnp.float32,
    )
    high = combined.astype(jnp.bfloat16)
    table[:kept] = high
    table[kept:] = (combined - high.astype(jnp.float32)).astype(jnp.bfloat16)

    pl.semaphore_wait(barrier, jnp.where(is_mid, owners + 1, owners))

    def tail_copy():
        return pltpu.make_async_remote_copy(
            src_ref=records.at[:, pl.ds(windows * WL - LEFT, LEFT)], dst_ref=halo,
            send_sem=halo_send, recv_sem=halo_recv,
            device_id={"win": lax.rem(me + 1, owners)}, device_id_type=MESH,
        )

    @pl.when(me < owners - 1)
    def _():
        tail_copy().start()

    def whiten_window(place, segment):
        both = lax.dot_general(
            table[...], segment, (((1,), (1,)), ((), ())), preferred_element_type=jnp.float32
        )
        stacked = both[:kept] + both[kept:]
        power = jnp.mean(stacked * stacked, axis=0, keepdims=True) + 1e-06
        whitened = stacked * (1.0 / jnp.sqrt(power))
        for lane in range(lanes):
            spectra[lane, pl.ds(place * kept, kept)] = whitened[:, lane * 128 : lane * 128 + 128]

    def whiten_group(turn):
        g = lax.rem(turn + 1, groups)
        base = g * span

        @pl.when(turn == 0)
        def _():
            load(0).wait()

        @pl.when(g > 0)
        def _():
            load(g).wait()
            whiten_window(0, rec[:, pl.ds(pl.multiple_of(base - LEFT, LEFT), LEFT + WL)])

        @pl.when(jnp.logical_and(g == 0, me == 0))
        def _():
            halo[...] = jnp.zeros_like(halo)

        @pl.when(jnp.logical_and(g == 0, me > 0))
        def _():
            pltpu.make_async_copy(halo, halo, halo_recv).wait()

        @pl.when(g == 0)
        def _():
            whiten_window(0, jnp.concatenate([halo[...], rec[:, :WL]], axis=1))

        for place in range(1, GROUP):
            start = pl.multiple_of(base + place * WL - LEFT, LEFT)
            whiten_window(place, rec[:, pl.ds(start, LEFT + WL)])

    mine = pl.ds(pl.multiple_of(me * unit, unit), unit)

    def start_block(n):
        pair = lax.rem(n, pairs)

        @pl.when(pair == 0)
        def _():
            whiten_group(n // pairs)

        for b in range(PER_CHUNK):
            for owner in range(owners):
                first = ((pair * PER_CHUNK + b) * owners + owner) * 2
                for lane in range(lanes):
                    real = spectra[lane, pl.ds(first, GROUP, stride=kept)]
                    imag = spectra[lane, pl.ds(first + 1, GROUP, stride=kept)]
                    x[n, owner, b, :, lane * 128 : lane * 128 + 128] = jnp.concatenate(
                        [real, imag], axis=0
                    ).astype(jnp.bfloat16)
        for step in range(1, owners):
            target = lax.rem(me + step, owners)
            pltpu.make_async_remote_copy(
                src_ref=x.at[n, target], dst_ref=own.at[n, :, mine],
                send_sem=a2a_send.at[n], recv_sem=a2a_recv.at[n],
                device_id={"win": target}, device_id_type=MESH,
            ).start()
        own[n, :, mine] = x[n, me]

    others = pl.ds(0, (owners - 1) * unit)

    def arrived(n):
        pltpu.make_async_copy(own.at[n, :, others], own.at[n, :, others], a2a_recv.at[n]).wait()

    def along(source, slot, n, which, target):
        return pltpu.make_async_remote_copy(
            src_ref=source.at[n], dst_ref=recv.at[slot, n],
            send_sem=z_send.at[which, n], recv_sem=z_recv.at[slot, n],
            device_id={"chan": target}, device_id_type=MESH,
        )

    def got(slot, n):
        pltpu.make_async_copy(recv.at[slot, n], recv.at[slot, n], z_recv.at[slot, n]).wait()

    def flush(pair):
        place = pl.ds(pair * PER_CHUNK, PER_CHUNK)
        return pltpu.make_async_copy(result.at[place], out.at[place], out_sem.at[pair])

    def multiply(n, choose):
        pair = lax.rem(n, pairs)
        started = n >= pairs
        for b in range(PER_CHUNK):
            at = pair * PER_CHUNK + b
            mine_now = own[n, b]
            depth, channels = mine_now.shape
            held = mine_now.astype(jnp.float32).reshape(owners, unit, channels)
            turned = jnp.concatenate([held[:, GROUP:], -held[:, :GROUP]], axis=1)
            turned = turned.astype(jnp.bfloat16).reshape(depth, channels)
            for index in range(ROUNDS):
                partner = choose(index, b)
                for part, right in enumerate((mine_now, turned)):
                    product = lax.dot_general(
                        partner, right, (((0,), (0,)), ((), ())),
                        preferred_element_type=jnp.float32,
                    )
                    total = jnp.where(started, acc[at, index, part], 0.0) + product
                    acc[at, index, part] = total
                    result[at, index, part] = (total * scale).astype(result.dtype)

        @pl.when(n >= chunks - pairs)
        def _():
            flush(pair).start()

    def when_in(step, lag, body):
        n = step - lag

        @pl.when(jnp.logical_and(n >= 0, n < chunks))
        def _():
            body(n)

    keys = [plan[index, 0] for index in range(ROUNDS)]
    has_1 = jnp.logical_or(keys[0] == 1, keys[1] == 1)
    has_3 = jnp.logical_or(keys[0] == 3, keys[1] == 3)

    @pl.when(is_mid)
    def _():
        def take_own(n):
            arrived(n)
            along(own, 1, n, 0, inner).start()

        def take_outer(n):
            got(0, n)
            along(recv.at[0], 2, n, 1, inner).start()

        def take_inner(n):
            got(1, n)
            stage[0, n] = jnp.where(has_1, own[n], recv[1, n])
            along(stage.at[0], 0, n, 2, outer).start()

        def take_far(n):
            got(2, n)
            stage[1, n] = jnp.where(has_3, recv[2, n], recv[1, n])
            along(stage.at[1], 1, n, 3, outer).start()

        def multiply_mid(n):
            def choose(index, b):
                key = keys[index]
                later = jnp.where(key == 3, recv[1, n, b], recv[2, n, b])
                return jnp.where(key == 1, recv[0, n, b], later)

            multiply(n, choose)

        def step_mid(step, carry):
            when_in(step, LEAD, take_own)
            when_in(step, LEAD + 1, take_outer)
            when_in(step, LEAD + 2, take_inner)
            when_in(step, LEAD + 4, take_far)
            when_in(step, 0, start_block)
            when_in(step, LEAD + 4, multiply_mid)
            return carry

        lax.fori_loop(0, chunks + LEAD + 4, step_mid, 0)

        def finish(n, carry):
            along(own, 1, n, 0, inner).wait_send()
            along(recv.at[0], 2, n, 1, inner).wait_send()
            along(stage.at[0], 0, n, 2, outer).wait_send()
            along(stage.at[1], 1, n, 3, outer).wait_send()
            return carry

        lax.fori_loop(0, chunks, finish, 0)

    @pl.when(is_end)
    def _():
        def take_own(n):
            arrived(n)
            along(own, 0, n, 0, next_in).start()

        def take_both(n):
            got(0, n)
            got(1, n)

            def choose(index, b):
                key = keys[index]
                in_first = jnp.logical_or(
                    key == 1, jnp.logical_and(key == 2, jnp.logical_not(has_1))
                )
                return jnp.where(in_first, recv[0, n, b], recv[1, n, b])

            multiply(n, choose)

        def step_end(step, carry):
            when_in(step, LEAD, take_own)
            when_in(step, 0, start_block)
            when_in(step, LEAD + 7, take_both)
            return carry

        lax.fori_loop(0, chunks + LEAD + 7, step_end, 0)

        def finish(n, carry):
            along(own, 0, n, 0, next_in).wait_send()
            return carry

        lax.fori_loop(0, chunks, finish, 0)

    def finish_all(n, carry):
        pltpu.make_async_copy(own.at[n, :, others], own.at[n, :, others], a2a_send.at[n]).wait()
        return carry

    lax.fori_loop(0, chunks, finish_all, 0)

    for pair in range(pairs):
        flush(pair).wait()

    @pl.when(me < owners - 1)
    def _():
        tail_copy().wait_send()


def exchange(records, fir_taps, plan, scale):
    channels, samples_here = records.shape
    owners = lax.axis_size("win")
    bins, windows = F // owners, samples_here // WL
    chunks = (windows // GROUP) * (bins // PER_CHUNK)
    block = (chunks, PER_CHUNK, owners * 2 * GROUP, channels)
    in_place = pl.BlockSpec(memory_space=pl.ANY)
    result = (bins, ROUNDS, 2, channels, channels)
    return pl.pallas_call(
        functools.partial(exchange_kernel, owners, bins, windows, scale),
        out_shape=jax.ShapeDtypeStruct(result, jnp.bfloat16),
        in_specs=[in_place] * 4,
        out_specs=in_place,
        scratch_shapes=[
            pltpu.SMEM(plan.shape, jnp.int32),
            pltpu.VMEM((1, TAPS), jnp.float32),
            pltpu.VMEM((2 * F, WL), jnp.float32),
            pltpu.VMEM(records.shape, jnp.bfloat16),
            pltpu.VMEM((4 * F, LEFT + WL), jnp.bfloat16),
            pltpu.VMEM((channels, LEFT), jnp.bfloat16),
            pltpu.VMEM((channels // 128, GROUP * 2 * F, 128), jnp.float32),
            pltpu.VMEM((chunks, owners, PER_CHUNK, 2 * GROUP, channels), jnp.bfloat16),
            pltpu.VMEM(block, jnp.bfloat16),
            pltpu.VMEM((3,) + block, jnp.bfloat16),
            pltpu.VMEM((2,) + block, jnp.bfloat16),
            pltpu.VMEM(result, jnp.float32),
            pltpu.VMEM(result, jnp.bfloat16),
            pltpu.SemaphoreType.DMA((3,)),
            pltpu.SemaphoreType.DMA((windows // GROUP,)),
            pltpu.SemaphoreType.DMA,
            pltpu.SemaphoreType.DMA,
            pltpu.SemaphoreType.DMA((chunks,)),
            pltpu.SemaphoreType.DMA((chunks,)),
            pltpu.SemaphoreType.DMA((4, chunks)),
            pltpu.SemaphoreType.DMA((3, chunks)),
            pltpu.SemaphoreType.DMA((bins // PER_CHUNK,)),
        ],
        compiler_params=pltpu.CompilerParams(
            collective_id=0, has_side_effects=True, vmem_limit_bytes=48 * 1024 * 1024
        ),
        name="exchange",
    )(plan, records, fir_taps[None, :], jnp.asarray(dft_rows(owners)))


def cross_kernel(scale, groups, rows, slots, own, first, second, out):
    half = rows // 2
    depth, channels = own.shape
    held = own[...].astype(jnp.float32).reshape(groups, rows, channels)
    turned = jnp.concatenate([held[:, half:], -held[:, :half]], axis=1)
    turned = turned.astype(jnp.bfloat16).reshape(depth, channels)
    for index, partner in enumerate((first, second)):
        for part, right in enumerate((own[...], turned)):
            product = lax.dot_general(
                partner[...], right, (((0,), (0,)), ((), ())), preferred_element_type=jnp.float32
            )
            out[index, part] = product * scale


def cross_terms(gathered, slots, groups, scale):
    _, bins, depth, channels = gathered.shape
    taken = lambda which: pl.BlockSpec(
        (None, None, depth, channels), lambda m, s: (s[which], m, 0, 0)
    )
    return pl.pallas_call(
        functools.partial(cross_kernel, scale, groups, depth // groups),
        out_shape=jax.ShapeDtypeStruct((bins, ROUNDS, 2, channels, channels), jnp.float32),
        grid_spec=pltpu.PrefetchScalarGridSpec(
            num_scalar_prefetch=1,
            grid=(bins,),
            in_specs=[
                pl.BlockSpec((None, None, depth, channels), lambda m, s: (0, m, 0, 0)),
                taken(0),
                taken(1),
            ],
            out_specs=pl.BlockSpec(
                (None, ROUNDS, 2, channels, channels), lambda m, s: (m, 0, 0, 0, 0)
            ),
        ),
        compiler_params=pltpu.CompilerParams(
            dimension_semantics=("arbitrary",), vmem_limit_bytes=40 * 1024 * 1024
        ),
        name="cross",
    )(slots, gathered, gathered, gathered)


def gather_images(x):
    owners, bins, rows, channels = x.shape
    swapped = lax.all_to_all(x, "win", 0, 0, tiled=True)
    images = [swapped.transpose(1, 0, 2, 3).reshape(bins, owners * rows, channels)]
    for bit_place in range(lax.axis_size("chan").bit_length() - 1):
        images = images + [from_partner(image, "chan", bit_place) for image in images]
    return jnp.stack(images)


def on_device(records, fir_taps, plan):
    channels, samples_here = records.shape
    window_count = samples_here // WL
    owners = lax.axis_size("win")
    chan = lax.axis_index("chan")
    scale = 1.0 / math.sqrt(window_count * owners)
    keys = jnp.bitwise_xor(plan[:, chan], chan)
    if lax.axis_size("chan") == 4:
        return exchange(records, fir_taps, plan, scale).astype(jnp.float32)
    whitened = whiten(records, fir_taps)
    gathered = gather_images(
        whitened.reshape(owners, F // owners, 2 * window_count, channels)
    )
    return cross_terms(gathered, keys.astype(jnp.int32), owners, scale)


def solution(mesh):
    placed = (P("chan", "win"), P(), P())
    return jax.shard_map(
        on_device,
        mesh=mesh,
        in_specs=placed,
        out_specs=P("win", None, None, None, "chan"),
        check_vma=False,
    )
```

```python
import functools
import math

import jax
import jax.numpy as jnp
import numpy as np
from jax import lax
from jax.experimental import pallas as pl
from jax.experimental.pallas import tpu as pltpu
from jax.sharding import PartitionSpec as P

WL = 256
F = 64
TAPS = 64
ROUNDS = 2
LEFT = 128
GROUP = 8
PER_CHUNK = 1
LEAD = 2
SETTLE = LEAD + 12
MESH = pl.DeviceIdType.MESH


def shifted(array, axis, by):
    count = lax.axis_size(axis)
    pairs = [(i, i + by) for i in range(count) if 0 <= i + by < count]
    return lax.ppermute(array, axis, pairs)


def from_partner(block, axis, bit):
    count = lax.axis_size(axis)
    route = []
    for low in range(count):
        high = low | 1 << bit
        if high != low and high < count:
            route += [(low, high), (high, low)]
    return lax.ppermute(block, axis, route)


def fir_matrix(fir_taps):
    inputs_at = jnp.arange(WL + TAPS - 1, dtype=jnp.int32)[:, None]
    outputs_at = jnp.arange(WL, dtype=jnp.int32)[None, :]
    tap_number = outputs_at + (TAPS - 1) - inputs_at
    inside = (tap_number >= 0) & (tap_number < TAPS)
    picked = fir_taps[jnp.clip(tap_number, 0, TAPS - 1)]
    return jnp.where(inside, picked, jnp.zeros_like(picked))


def dft_table():
    sample_at = jnp.arange(WL, dtype=jnp.int32)[:, None]
    column_at = jnp.arange(2 * F, dtype=jnp.int32)[None, :]
    bin_number = column_at // 2 + 1
    phases = (sample_at * bin_number % WL).astype(jnp.float32) * (2.0 * math.pi / WL)
    return jnp.where(column_at % 2 == 0, jnp.cos(phases), -jnp.sin(phases))


def split_table(fir_taps):
    table = jnp.dot(fir_matrix(fir_taps), dft_table(), precision=lax.Precision.HIGHEST)
    high = table.astype(jnp.bfloat16)
    low = (table - high.astype(jnp.float32)).astype(jnp.bfloat16)
    return jnp.concatenate([high, low], axis=1)


def whiten(records, fir_taps):
    channels, samples_here = records.shape
    window_count = samples_here // WL
    previous_tail = shifted(records[:, samples_here - TAPS + 1 :], "win", 1)
    samples = records.reshape(channels, window_count, WL)
    previous = jnp.concatenate(
        [previous_tail[:, None, :], samples[:, :-1, WL - TAPS + 1 :]], axis=1
    )
    table = split_table(fir_taps)
    both = jnp.einsum(
        "cwi,ik->kwc", samples, table[TAPS - 1 :], preferred_element_type=jnp.float32
    )
    both = both + jnp.einsum(
        "cwi,ik->kwc", previous, table[: TAPS - 1], preferred_element_type=jnp.float32
    )
    stacked = both[: 2 * F] + both[2 * F :]
    band_power = jnp.mean(stacked * stacked, axis=0, keepdims=True) + 1e-06
    return (stacked / jnp.sqrt(band_power)).astype(jnp.bfloat16)


def dft_rows(owners):
    bins = F // owners
    place = np.arange(bins)[:, None, None]
    owner = np.arange(owners)[None, :, None]
    part = np.arange(2)[None, None, :]
    number = np.broadcast_to(owner * bins + place + 1, (bins, owners, 2)).reshape(-1, 1)
    part = np.broadcast_to(part, (bins, owners, 2)).reshape(-1, 1)
    phases = (np.arange(WL)[None, :] * number % WL) * (2.0 * np.pi / WL)
    return np.where(part == 0, np.cos(phases), -np.sin(phases)).astype(np.float32)


def exchange_kernel(owners, bins, windows, scale, plan_at, records, taps_at, dft_at, out,
                    plan, taps, dft, rec, table, halo, spectra, x, own, recv, stage, acc, result,
                    small_sem, rec_sem, halo_send, halo_recv, a2a_send, a2a_recv, z_send, z_recv, out_sem):
    chan = lax.axis_index("chan")
    me = lax.axis_index("win")
    is_mid = jnp.logical_and(chan >= 1, chan <= 2)
    is_end = jnp.logical_not(is_mid)
    inner = 3 - chan
    outer = 3 * (chan - 1)
    next_in = 1 + chan // 3
    kept = 2 * F
    lanes = spectra.shape[0]
    groups = windows // GROUP
    pairs = bins // PER_CHUNK
    chunks = groups * pairs
    span = GROUP * WL
    unit = 2 * GROUP

    def load(g):
        columns = pl.ds(pl.multiple_of(g * span, span), span)
        return pltpu.make_async_copy(records.at[:, columns], rec.at[:, columns], rec_sem.at[g])

    small = [
        pltpu.make_async_copy(source, target, small_sem.at[place])
        for place, (source, target) in enumerate(((taps_at, taps), (dft_at, dft), (plan_at, plan)))
    ]
    for copy in small:
        copy.start()
    for g in range(groups):
        load(g).start()

    barrier = pltpu.get_barrier_semaphore()
    for step in range(1, owners):
        pl.semaphore_signal(barrier, inc=1, device_id={"win": lax.rem(me + step, owners)}, device_id_type=MESH)

    @pl.when(is_mid)
    def _():
        pl.semaphore_signal(barrier, inc=1, device_id={"chan": inner}, device_id_type=MESH)
        pl.semaphore_signal(barrier, inc=1, device_id={"chan": outer}, device_id_type=MESH)

    @pl.when(is_end)
    def _():
        pl.semaphore_signal(barrier, inc=1, device_id={"chan": next_in}, device_id_type=MESH)

    for copy in small:
        copy.wait()
    row = jnp.concatenate([taps[...], jnp.zeros((1, LEFT + WL + LEFT - TAPS), jnp.float32)], axis=1)
    spread = jnp.broadcast_to(row, (LEFT + WL, LEFT + WL + LEFT))
    shifted_taps = pltpu.roll(spread, 0, 1, stride=1, stride_axis=0)[:, LEFT : LEFT + WL]
    combined = lax.dot_general(
        dft[...], shifted_taps, (((1,), (1,)), ((), ())),
        precision=lax.Precision.HIGHEST, preferred_element_type=jnp.float32,
    )
    high = combined.astype(jnp.bfloat16)
    table[:kept] = high
    table[kept:] = (combined - high.astype(jnp.float32)).astype(jnp.bfloat16)

    pl.semaphore_wait(barrier, jnp.where(is_mid, owners + 1, owners))

    def tail_copy():
        return pltpu.make_async_remote_copy(
            src_ref=records.at[:, pl.ds(windows * WL - LEFT, LEFT)], dst_ref=halo,
            send_sem=halo_send, recv_sem=halo_recv,
            device_id={"win": lax.rem(me + 1, owners)}, device_id_type=MESH,
        )

    @pl.when(me < owners - 1)
    def _():
        tail_copy().start()

    def whiten_window(place, segment):
        both = lax.dot_general(
            table[...], segment, (((1,), (1,)), ((), ())), preferred_element_type=jnp.float32
        )
        stacked = both[:kept] + both[kept:]
        power = jnp.mean(stacked * stacked, axis=0, keepdims=True) + 1e-06
        whitened = stacked * (1.0 / jnp.sqrt(power))
        for lane in range(lanes):
            spectra[lane, pl.ds(place * kept, kept)] = whitened[:, lane * 128 : lane * 128 + 128]

    def whiten_group(turn):
        g = lax.rem(turn + 1, groups)
        base = g * span

        @pl.when(turn == 0)
        def _():
            load(0).wait()

        @pl.when(g > 0)
        def _():
            load(g).wait()
            whiten_window(0, rec[:, pl.ds(pl.multiple_of(base - LEFT, LEFT), LEFT + WL)])

        @pl.when(jnp.logical_and(g == 0, me == 0))
        def _():
            halo[...] = jnp.zeros_like(halo)

        @pl.when(jnp.logical_and(g == 0, me > 0))
        def _():
            pltpu.make_async_copy(halo, halo, halo_recv).wait()

        @pl.when(g == 0)
        def _():
            whiten_window(0, jnp.concatenate([halo[...], rec[:, :WL]], axis=1))

        for place in range(1, GROUP):
            start = pl.multiple_of(base + place * WL - LEFT, LEFT)
            whiten_window(place, rec[:, pl.ds(start, LEFT + WL)])

    mine = pl.ds(pl.multiple_of(me * unit, unit), unit)

    def start_block(n):
        pair = lax.rem(n, pairs)

        @pl.when(pair == 0)
        def _():
            whiten_group(n // pairs)

        for b in range(PER_CHUNK):
            for owner in range(owners):
                first = ((pair * PER_CHUNK + b) * owners + owner) * 2
                for lane in range(lanes):
                    real = spectra[lane, pl.ds(first, GROUP, stride=kept)]
                    imag = spectra[lane, pl.ds(first + 1, GROUP, stride=kept)]
                    x[n, owner, b, :, lane * 128 : lane * 128 + 128] = jnp.concatenate(
                        [real, imag], axis=0
                    ).astype(jnp.bfloat16)
        for step in range(1, owners):
            target = lax.rem(me + step, owners)
            pltpu.make_async_remote_copy(
                src_ref=x.at[n, target], dst_ref=own.at[n, :, mine],
                send_sem=a2a_send.at[n], recv_sem=a2a_recv.at[n],
                device_id={"win": target}, device_id_type=MESH,
            ).start()
        own[n, :, mine] = x[n, me]

    others = pl.ds(0, (owners - 1) * unit)

    def arrived(n):
        pltpu.make_async_copy(own.at[n, :, others], own.at[n, :, others], a2a_recv.at[n]).wait()

    def along(source, slot, n, which, target):
        return pltpu.make_async_remote_copy(
            src_ref=source.at[n], dst_ref=recv.at[slot, n],
            send_sem=z_send.at[which, n], recv_sem=z_recv.at[slot, n],
            device_id={"chan": target}, device_id_type=MESH,
        )

    def got(slot, n):
        pltpu.make_async_copy(recv.at[slot, n], recv.at[slot, n], z_recv.at[slot, n]).wait()

    def flush(pair):
        place = pl.ds(pair * PER_CHUNK, PER_CHUNK)
        return pltpu.make_async_copy(result.at[place], out.at[place], out_sem.at[pair])

    def multiply(n, choose):
        pair = lax.rem(n, pairs)
        started = n >= pairs
        for b in range(PER_CHUNK):
            at = pair * PER_CHUNK + b
            mine_now = own[n, b]
            depth, channels = mine_now.shape
            held = mine_now.astype(jnp.float32).reshape(owners, unit, channels)
            turned = jnp.concatenate([held[:, GROUP:], -held[:, :GROUP]], axis=1)
            turned = turned.astype(jnp.bfloat16).reshape(depth, channels)
            for index in range(ROUNDS):
                partner = choose(index, b)
                for part, right in enumerate((mine_now, turned)):
                    product = lax.dot_general(
                        partner, right, (((0,), (0,)), ((), ())),
                        preferred_element_type=jnp.float32,
                    )
                    total = jnp.where(started, acc[at, index, part], 0.0) + product
                    acc[at, index, part] = total
                    result[at, index, part] = (total * scale).astype(result.dtype)

        @pl.when(n >= chunks - pairs)
        def _():
            flush(pair).start()

    def when_in(step, lag, body):
        n = step - lag

        @pl.when(jnp.logical_and(n >= 0, n < chunks))
        def _():
            body(n)

    def sent(n):
        pltpu.make_async_copy(own.at[n, :, others], own.at[n, :, others], a2a_send.at[n]).wait()

    def run(steps, body, finish):
        lax.fori_loop(0, steps, body, 0)

        def rest(n, carry):
            finish(n)
            return carry

        lax.fori_loop(steps - SETTLE, chunks, rest, 0)

    keys = [plan[index, 0] for index in range(ROUNDS)]
    has_1 = jnp.logical_or(keys[0] == 1, keys[1] == 1)
    has_3 = jnp.logical_or(keys[0] == 3, keys[1] == 3)

    @pl.when(is_mid)
    def _():
        def take_own(n):
            arrived(n)
            along(own, 1, n, 0, inner).start()

        def take_outer(n):
            got(0, n)
            along(recv.at[0], 2, n, 1, inner).start()

        def take_inner(n):
            got(1, n)
            stage[0, n] = jnp.where(has_1, own[n], recv[1, n])
            along(stage.at[0], 0, n, 2, outer).start()

        def take_far(n):
            got(2, n)
            stage[1, n] = jnp.where(has_3, recv[2, n], recv[1, n])
            along(stage.at[1], 1, n, 3, outer).start()

        def multiply_mid(n):
            def choose(index, b):
                key = keys[index]
                later = jnp.where(key == 3, recv[1, n, b], recv[2, n, b])
                return jnp.where(key == 1, recv[0, n, b], later)

            multiply(n, choose)

        def finish(n):
            sent(n)
            along(own, 1, n, 0, inner).wait_send()
            along(recv.at[0], 2, n, 1, inner).wait_send()
            along(stage.at[0], 0, n, 2, outer).wait_send()
            along(stage.at[1], 1, n, 3, outer).wait_send()

        def step_mid(step, carry):
            when_in(step, LEAD, take_own)
            when_in(step, LEAD + 2, take_inner)
            when_in(step, LEAD + 2, take_outer)
            when_in(step, LEAD + 4, take_far)
            when_in(step, 0, start_block)
            when_in(step, LEAD + 4, multiply_mid)
            when_in(step, SETTLE, finish)
            return carry

        run(chunks + LEAD + 4, step_mid, finish)

    @pl.when(is_end)
    def _():
        def take_own(n):
            arrived(n)
            along(own, 0, n, 0, next_in).start()

        def take_both(n):
            got(0, n)
            got(1, n)

            def choose(index, b):
                key = keys[index]
                in_first = jnp.logical_or(
                    key == 1, jnp.logical_and(key == 2, jnp.logical_not(has_1))
                )
                return jnp.where(in_first, recv[0, n, b], recv[1, n, b])

            multiply(n, choose)

        def finish(n):
            sent(n)
            along(own, 0, n, 0, next_in).wait_send()

        def step_end(step, carry):
            when_in(step, LEAD, take_own)
            when_in(step, 0, start_block)
            when_in(step, SETTLE, finish)
            when_in(step, LEAD + 7, take_both)
            return carry

        run(chunks + LEAD + 7, step_end, finish)


    for pair in range(pairs):
        flush(pair).wait()

    @pl.when(me < owners - 1)
    def _():
        tail_copy().wait_send()


def exchange(records, fir_taps, plan, scale):
    channels, samples_here = records.shape
    owners = lax.axis_size("win")
    bins, windows = F // owners, samples_here // WL
    chunks = (windows // GROUP) * (bins // PER_CHUNK)
    block = (chunks, PER_CHUNK, owners * 2 * GROUP, channels)
    in_place = pl.BlockSpec(memory_space=pl.ANY)
    result = (bins, ROUNDS, 2, channels, channels)
    return pl.pallas_call(
        functools.partial(exchange_kernel, owners, bins, windows, scale),
        out_shape=jax.ShapeDtypeStruct(result, jnp.bfloat16),
        in_specs=[in_place] * 4,
        out_specs=in_place,
        scratch_shapes=[
            pltpu.SMEM(plan.shape, jnp.int32),
            pltpu.VMEM((1, TAPS), jnp.float32),
            pltpu.VMEM((2 * F, WL), jnp.float32),
            pltpu.VMEM(records.shape, jnp.bfloat16),
            pltpu.VMEM((4 * F, LEFT + WL), jnp.bfloat16),
            pltpu.VMEM((channels, LEFT), jnp.bfloat16),
            pltpu.VMEM((channels // 128, GROUP * 2 * F, 128), jnp.float32),
            pltpu.VMEM((chunks, owners, PER_CHUNK, 2 * GROUP, channels), jnp.bfloat16),
            pltpu.VMEM(block, jnp.bfloat16),
            pltpu.VMEM((3,) + block, jnp.bfloat16),
            pltpu.VMEM((2,) + block, jnp.bfloat16),
            pltpu.VMEM(result, jnp.float32),
            pltpu.VMEM(result, jnp.bfloat16),
            pltpu.SemaphoreType.DMA((3,)),
            pltpu.SemaphoreType.DMA((windows // GROUP,)),
            pltpu.SemaphoreType.DMA,
            pltpu.SemaphoreType.DMA,
            pltpu.SemaphoreType.DMA((chunks,)),
            pltpu.SemaphoreType.DMA((chunks,)),
            pltpu.SemaphoreType.DMA((4, chunks)),
            pltpu.SemaphoreType.DMA((3, chunks)),
            pltpu.SemaphoreType.DMA((bins // PER_CHUNK,)),
        ],
        compiler_params=pltpu.CompilerParams(
            collective_id=0, has_side_effects=True, vmem_limit_bytes=48 * 1024 * 1024
        ),
        name="exchange",
    )(plan, records, fir_taps[None, :], jnp.asarray(dft_rows(owners)))


def cross_kernel(scale, groups, rows, slots, own, first, second, out):
    half = rows // 2
    depth, channels = own.shape
    held = own[...].astype(jnp.float32).reshape(groups, rows, channels)
    turned = jnp.concatenate([held[:, half:], -held[:, :half]], axis=1)
    turned = turned.astype(jnp.bfloat16).reshape(depth, channels)
    for index, partner in enumerate((first, second)):
        for part, right in enumerate((own[...], turned)):
            product = lax.dot_general(
                partner[...], right, (((0,), (0,)), ((), ())), preferred_element_type=jnp.float32
            )
            out[index, part] = product * scale


def cross_terms(gathered, slots, groups, scale):
    _, bins, depth, channels = gathered.shape
    taken = lambda which: pl.BlockSpec(
        (None, None, depth, channels), lambda m, s: (s[which], m, 0, 0)
    )
    return pl.pallas_call(
        functools.partial(cross_kernel, scale, groups, depth // groups),
        out_shape=jax.ShapeDtypeStruct((bins, ROUNDS, 2, channels, channels), jnp.float32),
        grid_spec=pltpu.PrefetchScalarGridSpec(
            num_scalar_prefetch=1,
            grid=(bins,),
            in_specs=[
                pl.BlockSpec((None, None, depth, channels), lambda m, s: (0, m, 0, 0)),
                taken(0),
                taken(1),
            ],
            out_specs=pl.BlockSpec(
                (None, ROUNDS, 2, channels, channels), lambda m, s: (m, 0, 0, 0, 0)
            ),
        ),
        compiler_params=pltpu.CompilerParams(
            dimension_semantics=("arbitrary",), vmem_limit_bytes=40 * 1024 * 1024
        ),
        name="cross",
    )(slots, gathered, gathered, gathered)


def gather_images(x):
    owners, bins, rows, channels = x.shape
    swapped = lax.all_to_all(x, "win", 0, 0, tiled=True)
    images = [swapped.transpose(1, 0, 2, 3).reshape(bins, owners * rows, channels)]
    for bit_place in range(lax.axis_size("chan").bit_length() - 1):
        images = images + [from_partner(image, "chan", bit_place) for image in images]
    return jnp.stack(images)


def on_device(records, fir_taps, plan):
    channels, samples_here = records.shape
    window_count = samples_here // WL
    owners = lax.axis_size("win")
    chan = lax.axis_index("chan")
    scale = 1.0 / math.sqrt(window_count * owners)
    keys = jnp.bitwise_xor(plan[:, chan], chan)
    if lax.axis_size("chan") == 4:
        return exchange(records, fir_taps, plan, scale).astype(jnp.float32)
    whitened = whiten(records, fir_taps)
    gathered = gather_images(
        whitened.reshape(owners, F // owners, 2 * window_count, channels)
    )
    return cross_terms(gathered, keys.astype(jnp.int32), owners, scale)


def solution(mesh):
    placed = (P("chan", "win"), P(), P())
    return jax.shard_map(
        on_device,
        mesh=mesh,
        in_specs=placed,
        out_specs=P("win", None, None, None, "chan"),
        check_vma=False,
    )
```

```python
import functools
import math

import jax
import jax.numpy as jnp
import numpy as np
from jax import lax
from jax.experimental import pallas as pl
from jax.experimental.pallas import tpu as pltpu
from jax.sharding import PartitionSpec as P

WL = 256
F = 64
TAPS = 64
ROUNDS = 2
LEFT = 128
GROUP = 8
PER_CHUNK = 1
LEAD = 2
SETTLE = LEAD + 12
MESH = pl.DeviceIdType.MESH


def shifted(array, axis, by):
    count = lax.axis_size(axis)
    pairs = [(i, i + by) for i in range(count) if 0 <= i + by < count]
    return lax.ppermute(array, axis, pairs)


def from_partner(block, axis, bit):
    count = lax.axis_size(axis)
    route = []
    for low in range(count):
        high = low | 1 << bit
        if high != low and high < count:
            route += [(low, high), (high, low)]
    return lax.ppermute(block, axis, route)


def fir_matrix(fir_taps):
    inputs_at = jnp.arange(WL + TAPS - 1, dtype=jnp.int32)[:, None]
    outputs_at = jnp.arange(WL, dtype=jnp.int32)[None, :]
    tap_number = outputs_at + (TAPS - 1) - inputs_at
    inside = (tap_number >= 0) & (tap_number < TAPS)
    picked = fir_taps[jnp.clip(tap_number, 0, TAPS - 1)]
    return jnp.where(inside, picked, jnp.zeros_like(picked))


def dft_table():
    sample_at = jnp.arange(WL, dtype=jnp.int32)[:, None]
    column_at = jnp.arange(2 * F, dtype=jnp.int32)[None, :]
    bin_number = column_at // 2 + 1
    phases = (sample_at * bin_number % WL).astype(jnp.float32) * (2.0 * math.pi / WL)
    return jnp.where(column_at % 2 == 0, jnp.cos(phases), -jnp.sin(phases))


def split_table(fir_taps):
    table = jnp.dot(fir_matrix(fir_taps), dft_table(), precision=lax.Precision.HIGHEST)
    high = table.astype(jnp.bfloat16)
    low = (table - high.astype(jnp.float32)).astype(jnp.bfloat16)
    return jnp.concatenate([high, low], axis=1)


def whiten(records, fir_taps):
    channels, samples_here = records.shape
    window_count = samples_here // WL
    previous_tail = shifted(records[:, samples_here - TAPS + 1 :], "win", 1)
    samples = records.reshape(channels, window_count, WL)
    previous = jnp.concatenate(
        [previous_tail[:, None, :], samples[:, :-1, WL - TAPS + 1 :]], axis=1
    )
    table = split_table(fir_taps)
    both = jnp.einsum(
        "cwi,ik->kwc", samples, table[TAPS - 1 :], preferred_element_type=jnp.float32
    )
    both = both + jnp.einsum(
        "cwi,ik->kwc", previous, table[: TAPS - 1], preferred_element_type=jnp.float32
    )
    stacked = both[: 2 * F] + both[2 * F :]
    band_power = jnp.mean(stacked * stacked, axis=0, keepdims=True) + 1e-06
    return (stacked / jnp.sqrt(band_power)).astype(jnp.bfloat16)


def dft_rows(owners):
    bins = F // owners
    place = np.arange(bins)[:, None, None]
    owner = np.arange(owners)[None, :, None]
    part = np.arange(2)[None, None, :]
    number = np.broadcast_to(owner * bins + place + 1, (bins, owners, 2)).reshape(-1, 1)
    part = np.broadcast_to(part, (bins, owners, 2)).reshape(-1, 1)
    phases = (np.arange(WL)[None, :] * number % WL) * (2.0 * np.pi / WL)
    return np.where(part == 0, np.cos(phases), -np.sin(phases)).astype(np.float32)


def exchange_kernel(owners, bins, windows, scale, plan_at, records, taps_at, dft_at, out,
                    plan, taps, dft, rec, table, halo, spectra, x, own, recv, stage, acc, result,
                    small_sem, rec_sem, halo_send, halo_recv, a2a_send, a2a_recv, z_send, z_recv, out_sem):
    chan = lax.axis_index("chan")
    me = lax.axis_index("win")
    is_mid = jnp.logical_and(chan >= 1, chan <= 2)
    is_end = jnp.logical_not(is_mid)
    inner = 3 - chan
    outer = 3 * (chan - 1)
    next_in = 1 + chan // 3
    kept = 2 * F
    lanes = spectra.shape[0]
    groups = windows // GROUP
    pairs = bins // PER_CHUNK
    chunks = groups * pairs
    span = GROUP * WL
    unit = 2 * GROUP

    def load(g):
        columns = pl.ds(pl.multiple_of(g * span, span), span)
        return pltpu.make_async_copy(records.at[:, columns], rec.at[:, columns], rec_sem.at[g])

    small = [
        pltpu.make_async_copy(source, target, small_sem.at[place])
        for place, (source, target) in enumerate(((taps_at, taps), (dft_at, dft), (plan_at, plan)))
    ]
    for copy in small:
        copy.start()
    for g in range(groups):
        load(g).start()

    barrier = pltpu.get_barrier_semaphore()
    for step in range(1, owners):
        pl.semaphore_signal(barrier, inc=1, device_id={"win": lax.rem(me + step, owners)}, device_id_type=MESH)

    @pl.when(is_mid)
    def _():
        pl.semaphore_signal(barrier, inc=1, device_id={"chan": inner}, device_id_type=MESH)
        pl.semaphore_signal(barrier, inc=1, device_id={"chan": outer}, device_id_type=MESH)

    @pl.when(is_end)
    def _():
        pl.semaphore_signal(barrier, inc=1, device_id={"chan": next_in}, device_id_type=MESH)

    for copy in small:
        copy.wait()
    row = jnp.concatenate([taps[...], jnp.zeros((1, LEFT + WL + LEFT - TAPS), jnp.float32)], axis=1)
    spread = jnp.broadcast_to(row, (LEFT + WL, LEFT + WL + LEFT))
    shifted_taps = pltpu.roll(spread, 0, 1, stride=1, stride_axis=0)[:, LEFT : LEFT + WL]
    combined = lax.dot_general(
        dft[...], shifted_taps, (((1,), (1,)), ((), ())),
        precision=lax.Precision.HIGHEST, preferred_element_type=jnp.float32,
    )
    high = combined.astype(jnp.bfloat16)
    table[:kept] = high
    table[kept:] = (combined - high.astype(jnp.float32)).astype(jnp.bfloat16)

    def whiten_window(place, segment):
        both = lax.dot_general(
            table[...], segment, (((1,), (1,)), ((), ())), preferred_element_type=jnp.float32
        )
        stacked = both[:kept] + both[kept:]
        power = jnp.mean(stacked * stacked, axis=0, keepdims=True) + 1e-06
        whitened = stacked * (1.0 / jnp.sqrt(power))
        for lane in range(lanes):
            spectra[lane, pl.ds(place * kept, kept)] = whitened[:, lane * 128 : lane * 128 + 128]

    def whiten_group(turn):
        g = lax.rem(turn + 1, groups)
        base = g * span

        @pl.when(turn == 0)
        def _():
            load(0).wait()

        @pl.when(g > 0)
        def _():
            load(g).wait()
            whiten_window(0, rec[:, pl.ds(pl.multiple_of(base - LEFT, LEFT), LEFT + WL)])

        @pl.when(jnp.logical_and(g == 0, me == 0))
        def _():
            halo[...] = jnp.zeros_like(halo)

        @pl.when(jnp.logical_and(g == 0, me > 0))
        def _():
            pltpu.make_async_copy(halo, halo, halo_recv).wait()

        @pl.when(g == 0)
        def _():
            whiten_window(0, jnp.concatenate([halo[...], rec[:, :WL]], axis=1))

        for place in range(1, GROUP):
            start = pl.multiple_of(base + place * WL - LEFT, LEFT)
            whiten_window(place, rec[:, pl.ds(start, LEFT + WL)])

    whiten_group(jnp.int32(0))
    pl.semaphore_wait(barrier, jnp.where(is_mid, owners + 1, owners))

    def tail_copy():
        return pltpu.make_async_remote_copy(
            src_ref=records.at[:, pl.ds(windows * WL - LEFT, LEFT)], dst_ref=halo,
            send_sem=halo_send, recv_sem=halo_recv,
            device_id={"win": lax.rem(me + 1, owners)}, device_id_type=MESH,
        )

    @pl.when(me < owners - 1)
    def _():
        tail_copy().start()

    mine = pl.ds(pl.multiple_of(me * unit, unit), unit)

    def start_block(n):
        pair = lax.rem(n, pairs)

        @pl.when(jnp.logical_and(pair == 0, n > 0))
        def _():
            whiten_group(n // pairs)

        for b in range(PER_CHUNK):
            for owner in range(owners):
                first = ((pair * PER_CHUNK + b) * owners + owner) * 2
                for lane in range(lanes):
                    real = spectra[lane, pl.ds(first, GROUP, stride=kept)]
                    imag = spectra[lane, pl.ds(first + 1, GROUP, stride=kept)]
                    x[n, owner, b, :, lane * 128 : lane * 128 + 128] = jnp.concatenate(
                        [real, imag], axis=0
                    ).astype(jnp.bfloat16)
        for step in range(1, owners):
            target = lax.rem(me + step, owners)
            pltpu.make_async_remote_copy(
                src_ref=x.at[n, target], dst_ref=own.at[n, :, mine],
                send_sem=a2a_send.at[n], recv_sem=a2a_recv.at[n],
                device_id={"win": target}, device_id_type=MESH,
            ).start()
        own[n, :, mine] = x[n, me]

    others = pl.ds(0, (owners - 1) * unit)

    def arrived(n):
        pltpu.make_async_copy(own.at[n, :, others], own.at[n, :, others], a2a_recv.at[n]).wait()

    def along(source, slot, n, which, target):
        return pltpu.make_async_remote_copy(
            src_ref=source.at[n], dst_ref=recv.at[slot, n],
            send_sem=z_send.at[which, n], recv_sem=z_recv.at[slot, n],
            device_id={"chan": target}, device_id_type=MESH,
        )

    def got(slot, n):
        pltpu.make_async_copy(recv.at[slot, n], recv.at[slot, n], z_recv.at[slot, n]).wait()

    def flush(pair):
        place = pl.ds(pair * PER_CHUNK, PER_CHUNK)
        return pltpu.make_async_copy(result.at[place], out.at[place], out_sem.at[pair])

    def multiply(n, choose):
        pair = lax.rem(n, pairs)
        started = n >= pairs
        for b in range(PER_CHUNK):
            at = pair * PER_CHUNK + b
            mine_now = own[n, b]
            depth, channels = mine_now.shape
            held = mine_now.astype(jnp.float32).reshape(owners, unit, channels)
            turned = jnp.concatenate([held[:, GROUP:], -held[:, :GROUP]], axis=1)
            turned = turned.astype(jnp.bfloat16).reshape(depth, channels)
            for index in range(ROUNDS):
                partner = choose(index, b)
                for part, right in enumerate((mine_now, turned)):
                    product = lax.dot_general(
                        partner, right, (((0,), (0,)), ((), ())),
                        preferred_element_type=jnp.float32,
                    )
                    total = jnp.where(started, acc[at, index, part], 0.0) + product
                    acc[at, index, part] = total
                    result[at, index, part] = (total * scale).astype(result.dtype)

        @pl.when(n >= chunks - pairs)
        def _():
            flush(pair).start()

    def when_in(step, lag, body):
        n = step - lag

        @pl.when(jnp.logical_and(n >= 0, n < chunks))
        def _():
            body(n)

    def sent(n):
        pltpu.make_async_copy(own.at[n, :, others], own.at[n, :, others], a2a_send.at[n]).wait()

    def run(steps, body, finish):
        lax.fori_loop(0, steps, body, 0)

        def rest(n, carry):
            finish(n)
            return carry

        lax.fori_loop(steps - SETTLE, chunks, rest, 0)

    keys = [plan[index, 0] for index in range(ROUNDS)]
    has_1 = jnp.logical_or(keys[0] == 1, keys[1] == 1)
    has_3 = jnp.logical_or(keys[0] == 3, keys[1] == 3)

    @pl.when(is_mid)
    def _():
        def take_own(n):
            arrived(n)
            along(own, 1, n, 0, inner).start()

        def take_outer(n):
            got(0, n)
            along(recv.at[0], 2, n, 1, inner).start()

        def take_inner(n):
            got(1, n)
            stage[0, n] = jnp.where(has_1, own[n], recv[1, n])
            along(stage.at[0], 0, n, 2, outer).start()

        def take_far(n):
            got(2, n)
            stage[1, n] = jnp.where(has_3, recv[2, n], recv[1, n])
            along(stage.at[1], 1, n, 3, outer).start()

        def multiply_mid(n):
            def choose(index, b):
                key = keys[index]
                later = jnp.where(key == 3, recv[1, n, b], recv[2, n, b])
                return jnp.where(key == 1, recv[0, n, b], later)

            multiply(n, choose)

        def finish(n):
            sent(n)
            along(own, 1, n, 0, inner).wait_send()
            along(recv.at[0], 2, n, 1, inner).wait_send()
            along(stage.at[0], 0, n, 2, outer).wait_send()
            along(stage.at[1], 1, n, 3, outer).wait_send()

        def step_mid(step, carry):
            when_in(step, LEAD, take_own)
            when_in(step, LEAD + 2, take_inner)
            when_in(step, LEAD + 2, take_outer)
            when_in(step, LEAD + 4, take_far)
            when_in(step, 0, start_block)
            when_in(step, LEAD + 4, multiply_mid)
            when_in(step, SETTLE, finish)
            return carry

        run(chunks + LEAD + 4, step_mid, finish)

    @pl.when(is_end)
    def _():
        def take_own(n):
            arrived(n)
            along(own, 0, n, 0, next_in).start()

        def take_both(n):
            got(0, n)
            got(1, n)

            def choose(index, b):
                key = keys[index]
                in_first = jnp.logical_or(
                    key == 1, jnp.logical_and(key == 2, jnp.logical_not(has_1))
                )
                return jnp.where(in_first, recv[0, n, b], recv[1, n, b])

            multiply(n, choose)

        def finish(n):
            sent(n)
            along(own, 0, n, 0, next_in).wait_send()

        def step_end(step, carry):
            when_in(step, LEAD, take_own)
            when_in(step, 0, start_block)
            when_in(step, SETTLE, finish)
            when_in(step, LEAD + 7, take_both)
            return carry

        run(chunks + LEAD + 7, step_end, finish)


    for pair in range(pairs):
        flush(pair).wait()

    @pl.when(me < owners - 1)
    def _():
        tail_copy().wait_send()


def exchange(records, fir_taps, plan, scale):
    channels, samples_here = records.shape
    owners = lax.axis_size("win")
    bins, windows = F // owners, samples_here // WL
    chunks = (windows // GROUP) * (bins // PER_CHUNK)
    block = (chunks, PER_CHUNK, owners * 2 * GROUP, channels)
    in_place = pl.BlockSpec(memory_space=pl.ANY)
    result = (bins, ROUNDS, 2, channels, channels)
    return pl.pallas_call(
        functools.partial(exchange_kernel, owners, bins, windows, scale),
        out_shape=jax.ShapeDtypeStruct(result, jnp.bfloat16),
        in_specs=[in_place] * 4,
        out_specs=in_place,
        scratch_shapes=[
            pltpu.SMEM(plan.shape, jnp.int32),
            pltpu.VMEM((1, TAPS), jnp.float32),
            pltpu.VMEM((2 * F, WL), jnp.float32),
            pltpu.VMEM(records.shape, jnp.bfloat16),
            pltpu.VMEM((4 * F, LEFT + WL), jnp.bfloat16),
            pltpu.VMEM((channels, LEFT), jnp.bfloat16),
            pltpu.VMEM((channels // 128, GROUP * 2 * F, 128), jnp.float32),
            pltpu.VMEM((chunks, owners, PER_CHUNK, 2 * GROUP, channels), jnp.bfloat16),
            pltpu.VMEM(block, jnp.bfloat16),
            pltpu.VMEM((3,) + block, jnp.bfloat16),
            pltpu.VMEM((2,) + block, jnp.bfloat16),
            pltpu.VMEM(result, jnp.float32),
            pltpu.VMEM(result, jnp.bfloat16),
            pltpu.SemaphoreType.DMA((3,)),
            pltpu.SemaphoreType.DMA((windows // GROUP,)),
            pltpu.SemaphoreType.DMA,
            pltpu.SemaphoreType.DMA,
            pltpu.SemaphoreType.DMA((chunks,)),
            pltpu.SemaphoreType.DMA((chunks,)),
            pltpu.SemaphoreType.DMA((4, chunks)),
            pltpu.SemaphoreType.DMA((3, chunks)),
            pltpu.SemaphoreType.DMA((bins // PER_CHUNK,)),
        ],
        compiler_params=pltpu.CompilerParams(
            collective_id=0, has_side_effects=True, vmem_limit_bytes=63 * 1024 * 1024
        ),
        name="exchange",
    )(plan, records, fir_taps[None, :], jnp.asarray(dft_rows(owners)))


def cross_kernel(scale, groups, rows, slots, own, first, second, out):
    half = rows // 2
    depth, channels = own.shape
    held = own[...].astype(jnp.float32).reshape(groups, rows, channels)
    turned = jnp.concatenate([held[:, half:], -held[:, :half]], axis=1)
    turned = turned.astype(jnp.bfloat16).reshape(depth, channels)
    for index, partner in enumerate((first, second)):
        for part, right in enumerate((own[...], turned)):
            product = lax.dot_general(
                partner[...], right, (((0,), (0,)), ((), ())), preferred_element_type=jnp.float32
            )
            out[index, part] = product * scale


def cross_terms(gathered, slots, groups, scale):
    _, bins, depth, channels = gathered.shape
    taken = lambda which: pl.BlockSpec(
        (None, None, depth, channels), lambda m, s: (s[which], m, 0, 0)
    )
    return pl.pallas_call(
        functools.partial(cross_kernel, scale, groups, depth // groups),
        out_shape=jax.ShapeDtypeStruct((bins, ROUNDS, 2, channels, channels), jnp.float32),
        grid_spec=pltpu.PrefetchScalarGridSpec(
            num_scalar_prefetch=1,
            grid=(bins,),
            in_specs=[
                pl.BlockSpec((None, None, depth, channels), lambda m, s: (0, m, 0, 0)),
                taken(0),
                taken(1),
            ],
            out_specs=pl.BlockSpec(
                (None, ROUNDS, 2, channels, channels), lambda m, s: (m, 0, 0, 0, 0)
            ),
        ),
        compiler_params=pltpu.CompilerParams(
            dimension_semantics=("arbitrary",), vmem_limit_bytes=40 * 1024 * 1024
        ),
        name="cross",
    )(slots, gathered, gathered, gathered)


def gather_images(x):
    owners, bins, rows, channels = x.shape
    swapped = lax.all_to_all(x, "win", 0, 0, tiled=True)
    images = [swapped.transpose(1, 0, 2, 3).reshape(bins, owners * rows, channels)]
    for bit_place in range(lax.axis_size("chan").bit_length() - 1):
        images = images + [from_partner(image, "chan", bit_place) for image in images]
    return jnp.stack(images)


def on_device(records, fir_taps, plan):
    channels, samples_here = records.shape
    window_count = samples_here // WL
    owners = lax.axis_size("win")
    chan = lax.axis_index("chan")
    scale = 1.0 / math.sqrt(window_count * owners)
    keys = jnp.bitwise_xor(plan[:, chan], chan)
    if lax.axis_size("chan") == 4:
        return exchange(records, fir_taps, plan, scale).astype(jnp.float32)
    whitened = whiten(records, fir_taps)
    gathered = gather_images(
        whitened.reshape(owners, F // owners, 2 * window_count, channels)
    )
    return cross_terms(gathered, keys.astype(jnp.int32), owners, scale)


def solution(mesh):
    placed = (P("chan", "win"), P(), P())
    return jax.shard_map(
        on_device,
        mesh=mesh,
        in_specs=placed,
        out_specs=P("win", None, None, None, "chan"),
        check_vma=False,
    )
```

```python
import functools
import math

import jax
import jax.numpy as jnp
import numpy as np
from jax import lax
from jax.experimental import pallas as pl
from jax.experimental.pallas import tpu as pltpu
from jax.sharding import PartitionSpec as P

WL = 256
F = 64
TAPS = 64
ROUNDS = 2
LEFT = 128
GROUP = 8
PER_CHUNK = 1
LEAD = 2
SETTLE = LEAD + 12
MESH = pl.DeviceIdType.MESH


def shifted(array, axis, by):
    count = lax.axis_size(axis)
    pairs = [(i, i + by) for i in range(count) if 0 <= i + by < count]
    return lax.ppermute(array, axis, pairs)


def from_partner(block, axis, bit):
    count = lax.axis_size(axis)
    route = []
    for low in range(count):
        high = low | 1 << bit
        if high != low and high < count:
            route += [(low, high), (high, low)]
    return lax.ppermute(block, axis, route)


def fir_matrix(fir_taps):
    inputs_at = jnp.arange(WL + TAPS - 1, dtype=jnp.int32)[:, None]
    outputs_at = jnp.arange(WL, dtype=jnp.int32)[None, :]
    tap_number = outputs_at + (TAPS - 1) - inputs_at
    inside = (tap_number >= 0) & (tap_number < TAPS)
    picked = fir_taps[jnp.clip(tap_number, 0, TAPS - 1)]
    return jnp.where(inside, picked, jnp.zeros_like(picked))


def dft_table():
    sample_at = jnp.arange(WL, dtype=jnp.int32)[:, None]
    column_at = jnp.arange(2 * F, dtype=jnp.int32)[None, :]
    bin_number = column_at // 2 + 1
    phases = (sample_at * bin_number % WL).astype(jnp.float32) * (2.0 * math.pi / WL)
    return jnp.where(column_at % 2 == 0, jnp.cos(phases), -jnp.sin(phases))


def split_table(fir_taps):
    table = jnp.dot(fir_matrix(fir_taps), dft_table(), precision=lax.Precision.HIGHEST)
    high = table.astype(jnp.bfloat16)
    low = (table - high.astype(jnp.float32)).astype(jnp.bfloat16)
    return jnp.concatenate([high, low], axis=1)


def whiten(records, fir_taps):
    channels, samples_here = records.shape
    window_count = samples_here // WL
    previous_tail = shifted(records[:, samples_here - TAPS + 1 :], "win", 1)
    samples = records.reshape(channels, window_count, WL)
    previous = jnp.concatenate(
        [previous_tail[:, None, :], samples[:, :-1, WL - TAPS + 1 :]], axis=1
    )
    table = split_table(fir_taps)
    both = jnp.einsum(
        "cwi,ik->kwc", samples, table[TAPS - 1 :], preferred_element_type=jnp.float32
    )
    both = both + jnp.einsum(
        "cwi,ik->kwc", previous, table[: TAPS - 1], preferred_element_type=jnp.float32
    )
    stacked = both[: 2 * F] + both[2 * F :]
    band_power = jnp.mean(stacked * stacked, axis=0, keepdims=True) + 1e-06
    return (stacked / jnp.sqrt(band_power)).astype(jnp.bfloat16)


def dft_rows(owners):
    bins = F // owners
    place = np.arange(bins)[:, None, None]
    owner = np.arange(owners)[None, :, None]
    part = np.arange(2)[None, None, :]
    number = np.broadcast_to(owner * bins + place + 1, (bins, owners, 2)).reshape(-1, 1)
    part = np.broadcast_to(part, (bins, owners, 2)).reshape(-1, 1)
    phases = (np.arange(WL)[None, :] * number % WL) * (2.0 * np.pi / WL)
    return np.where(part == 0, np.cos(phases), -np.sin(phases)).astype(np.float32)


def exchange_kernel(owners, bins, windows, scale, plan_at, records, taps, dft, out,
                    plan, rec, table, halo, spectra, x, own, recv, stage, acc, result,
                    plan_sem, rec_sem, halo_send, halo_recv, a2a_send, a2a_recv, z_send, z_recv, out_sem):
    chan = lax.axis_index("chan")
    me = lax.axis_index("win")
    is_mid = jnp.logical_and(chan >= 1, chan <= 2)
    is_end = jnp.logical_not(is_mid)
    inner = 3 - chan
    outer = 3 * (chan - 1)
    next_in = 1 + chan // 3
    kept = 2 * F
    lanes = spectra.shape[0]
    groups = windows // GROUP
    pairs = bins // PER_CHUNK
    chunks = groups * pairs
    span = GROUP * WL
    unit = 2 * GROUP

    def load(g):
        columns = pl.ds(pl.multiple_of(g * span, span), span)
        return pltpu.make_async_copy(records.at[:, columns], rec.at[:, columns], rec_sem.at[g])

    plan_copy = pltpu.make_async_copy(plan_at, plan, plan_sem)
    plan_copy.start()
    for g in range(groups):
        load(g).start()

    barrier = pltpu.get_barrier_semaphore()
    for step in range(1, owners):
        pl.semaphore_signal(barrier, inc=1, device_id={"win": lax.rem(me + step, owners)}, device_id_type=MESH)

    @pl.when(is_mid)
    def _():
        pl.semaphore_signal(barrier, inc=1, device_id={"chan": inner}, device_id_type=MESH)
        pl.semaphore_signal(barrier, inc=1, device_id={"chan": outer}, device_id_type=MESH)

    @pl.when(is_end)
    def _():
        pl.semaphore_signal(barrier, inc=1, device_id={"chan": next_in}, device_id_type=MESH)

    row = jnp.concatenate([taps[...], jnp.zeros((1, LEFT + WL + LEFT - TAPS), jnp.float32)], axis=1)
    spread = jnp.broadcast_to(row, (LEFT + WL, LEFT + WL + LEFT))
    shifted_taps = pltpu.roll(spread, 0, 1, stride=1, stride_axis=0)[:, LEFT : LEFT + WL]
    combined = lax.dot_general(
        dft[...], shifted_taps, (((1,), (1,)), ((), ())),
        precision=lax.Precision.HIGHEST, preferred_element_type=jnp.float32,
    )
    high = combined.astype(jnp.bfloat16)
    table[:kept] = high
    table[kept:] = (combined - high.astype(jnp.float32)).astype(jnp.bfloat16)

    def whiten_window(place, segment):
        both = lax.dot_general(
            table[...], segment, (((1,), (1,)), ((), ())), preferred_element_type=jnp.float32
        )
        stacked = both[:kept] + both[kept:]
        power = jnp.mean(stacked * stacked, axis=0, keepdims=True) + 1e-06
        whitened = stacked * (1.0 / jnp.sqrt(power))
        for lane in range(lanes):
            spectra[lane, pl.ds(place * kept, kept)] = whitened[:, lane * 128 : lane * 128 + 128]

    def whiten_group(turn):
        g = lax.rem(turn + 1, groups)
        base = g * span

        @pl.when(turn == 0)
        def _():
            load(0).wait()

        @pl.when(g > 0)
        def _():
            load(g).wait()
            whiten_window(0, rec[:, pl.ds(pl.multiple_of(base - LEFT, LEFT), LEFT + WL)])

        @pl.when(jnp.logical_and(g == 0, me == 0))
        def _():
            halo[...] = jnp.zeros_like(halo)

        @pl.when(jnp.logical_and(g == 0, me > 0))
        def _():
            pltpu.make_async_copy(halo, halo, halo_recv).wait()

        @pl.when(g == 0)
        def _():
            whiten_window(0, jnp.concatenate([halo[...], rec[:, :WL]], axis=1))

        for place in range(1, GROUP):
            start = pl.multiple_of(base + place * WL - LEFT, LEFT)
            whiten_window(place, rec[:, pl.ds(start, LEFT + WL)])

    whiten_group(jnp.int32(0))
    pl.semaphore_wait(barrier, jnp.where(is_mid, owners + 1, owners))

    def tail_copy():
        return pltpu.make_async_remote_copy(
            src_ref=records.at[:, pl.ds(windows * WL - LEFT, LEFT)], dst_ref=halo,
            send_sem=halo_send, recv_sem=halo_recv,
            device_id={"win": lax.rem(me + 1, owners)}, device_id_type=MESH,
        )

    @pl.when(me < owners - 1)
    def _():
        tail_copy().start()

    mine = pl.ds(pl.multiple_of(me * unit, unit), unit)

    def start_block(n):
        pair = lax.rem(n, pairs)

        @pl.when(jnp.logical_and(pair == 0, n > 0))
        def _():
            whiten_group(n // pairs)

        for b in range(PER_CHUNK):
            for owner in range(owners):
                first = ((pair * PER_CHUNK + b) * owners + owner) * 2
                for lane in range(lanes):
                    real = spectra[lane, pl.ds(first, GROUP, stride=kept)]
                    imag = spectra[lane, pl.ds(first + 1, GROUP, stride=kept)]
                    x[n, owner, b, :, lane * 128 : lane * 128 + 128] = jnp.concatenate(
                        [real, imag], axis=0
                    ).astype(jnp.bfloat16)
        for step in range(1, owners):
            target = lax.rem(me + step, owners)
            pltpu.make_async_remote_copy(
                src_ref=x.at[n, target], dst_ref=own.at[n, :, mine],
                send_sem=a2a_send.at[n], recv_sem=a2a_recv.at[n],
                device_id={"win": target}, device_id_type=MESH,
            ).start()
        own[n, :, mine] = x[n, me]

    others = pl.ds(0, (owners - 1) * unit)

    def arrived(n):
        pltpu.make_async_copy(own.at[n, :, others], own.at[n, :, others], a2a_recv.at[n]).wait()

    def along(source, slot, n, which, target):
        return pltpu.make_async_remote_copy(
            src_ref=source.at[n], dst_ref=recv.at[slot, n],
            send_sem=z_send.at[which, n], recv_sem=z_recv.at[slot, n],
            device_id={"chan": target}, device_id_type=MESH,
        )

    def got(slot, n):
        pltpu.make_async_copy(recv.at[slot, n], recv.at[slot, n], z_recv.at[slot, n]).wait()

    def flush(pair):
        place = pl.ds(pair * PER_CHUNK, PER_CHUNK)
        return pltpu.make_async_copy(result.at[place], out.at[place], out_sem.at[pair])

    def multiply(n, choose):
        pair = lax.rem(n, pairs)
        started = n >= pairs
        for b in range(PER_CHUNK):
            at = pair * PER_CHUNK + b
            mine_now = own[n, b]
            depth, channels = mine_now.shape
            held = mine_now.astype(jnp.float32).reshape(owners, unit, channels)
            turned = jnp.concatenate([held[:, GROUP:], -held[:, :GROUP]], axis=1)
            turned = turned.astype(jnp.bfloat16).reshape(depth, channels)
            for index in range(ROUNDS):
                partner = choose(index, b)
                for part, right in enumerate((mine_now, turned)):
                    product = lax.dot_general(
                        partner, right, (((0,), (0,)), ((), ())),
                        preferred_element_type=jnp.float32,
                    )
                    total = jnp.where(started, acc[at, index, part], 0.0) + product
                    acc[at, index, part] = total
                    result[at, index, part] = (total * scale).astype(result.dtype)

        @pl.when(n >= chunks - pairs)
        def _():
            flush(pair).start()

    def when_in(step, lag, body):
        n = step - lag

        @pl.when(jnp.logical_and(n >= 0, n < chunks))
        def _():
            body(n)

    def sent(n):
        pltpu.make_async_copy(own.at[n, :, others], own.at[n, :, others], a2a_send.at[n]).wait()

    def run(steps, body, finish):
        lax.fori_loop(0, steps, body, 0)

        def rest(n, carry):
            finish(n)
            return carry

        lax.fori_loop(steps - SETTLE, chunks, rest, 0)

    plan_copy.wait()
    keys = [plan[index, 0] for index in range(ROUNDS)]
    has_1 = jnp.logical_or(keys[0] == 1, keys[1] == 1)
    has_3 = jnp.logical_or(keys[0] == 3, keys[1] == 3)

    @pl.when(is_mid)
    def _():
        def take_own(n):
            arrived(n)
            along(own, 1, n, 0, inner).start()

        def take_outer(n):
            got(0, n)
            along(recv.at[0], 2, n, 1, inner).start()

        def take_inner(n):
            got(1, n)
            stage[0, n] = jnp.where(has_1, own[n], recv[1, n])
            along(stage.at[0], 0, n, 2, outer).start()

        def take_far(n):
            got(2, n)
            stage[1, n] = jnp.where(has_3, recv[2, n], recv[1, n])
            along(stage.at[1], 1, n, 3, outer).start()

        def multiply_mid(n):
            def choose(index, b):
                key = keys[index]
                later = jnp.where(key == 3, recv[1, n, b], recv[2, n, b])
                return jnp.where(key == 1, recv[0, n, b], later)

            multiply(n, choose)

        def finish(n):
            sent(n)
            along(own, 1, n, 0, inner).wait_send()
            along(recv.at[0], 2, n, 1, inner).wait_send()
            along(stage.at[0], 0, n, 2, outer).wait_send()
            along(stage.at[1], 1, n, 3, outer).wait_send()

        def step_mid(step, carry):
            when_in(step, LEAD, take_own)
            when_in(step, LEAD + 2, take_inner)
            when_in(step, LEAD + 2, take_outer)
            when_in(step, LEAD + 4, take_far)
            when_in(step, 0, start_block)
            when_in(step, LEAD + 4, multiply_mid)
            when_in(step, SETTLE, finish)
            return carry

        run(chunks + LEAD + 4, step_mid, finish)

    @pl.when(is_end)
    def _():
        def take_own(n):
            arrived(n)
            along(own, 0, n, 0, next_in).start()

        def take_both(n):
            got(0, n)
            got(1, n)

            def choose(index, b):
                key = keys[index]
                in_first = jnp.logical_or(
                    key == 1, jnp.logical_and(key == 2, jnp.logical_not(has_1))
                )
                return jnp.where(in_first, recv[0, n, b], recv[1, n, b])

            multiply(n, choose)

        def finish(n):
            sent(n)
            along(own, 0, n, 0, next_in).wait_send()

        def step_end(step, carry):
            when_in(step, LEAD, take_own)
            when_in(step, 0, start_block)
            when_in(step, SETTLE, finish)
            when_in(step, LEAD + 7, take_both)
            return carry

        run(chunks + LEAD + 7, step_end, finish)


    for pair in range(pairs):
        flush(pair).wait()

    @pl.when(me < owners - 1)
    def _():
        tail_copy().wait_send()


def exchange(records, fir_taps, plan, scale):
    channels, samples_here = records.shape
    owners = lax.axis_size("win")
    bins, windows = F // owners, samples_here // WL
    chunks = (windows // GROUP) * (bins // PER_CHUNK)
    block = (chunks, PER_CHUNK, owners * 2 * GROUP, channels)
    in_place = pl.BlockSpec(memory_space=pl.ANY)
    in_vmem = pl.BlockSpec(memory_space=pltpu.VMEM)
    result = (bins, ROUNDS, 2, channels, channels)
    return pl.pallas_call(
        functools.partial(exchange_kernel, owners, bins, windows, scale),
        out_shape=jax.ShapeDtypeStruct(result, jnp.bfloat16),
        in_specs=[in_place, in_place, in_vmem, in_vmem],
        out_specs=in_place,
        scratch_shapes=[
            pltpu.SMEM(plan.shape, jnp.int32),
            pltpu.VMEM(records.shape, jnp.bfloat16),
            pltpu.VMEM((4 * F, LEFT + WL), jnp.bfloat16),
            pltpu.VMEM((channels, LEFT), jnp.bfloat16),
            pltpu.VMEM((channels // 128, GROUP * 2 * F, 128), jnp.float32),
            pltpu.VMEM((chunks, owners, PER_CHUNK, 2 * GROUP, channels), jnp.bfloat16),
            pltpu.VMEM(block, jnp.bfloat16),
            pltpu.VMEM((3,) + block, jnp.bfloat16),
            pltpu.VMEM((2,) + block, jnp.bfloat16),
            pltpu.VMEM(result, jnp.float32),
            pltpu.VMEM(result, jnp.bfloat16),
            pltpu.SemaphoreType.DMA,
            pltpu.SemaphoreType.DMA((windows // GROUP,)),
            pltpu.SemaphoreType.DMA,
            pltpu.SemaphoreType.DMA,
            pltpu.SemaphoreType.DMA((chunks,)),
            pltpu.SemaphoreType.DMA((chunks,)),
            pltpu.SemaphoreType.DMA((4, chunks)),
            pltpu.SemaphoreType.DMA((3, chunks)),
            pltpu.SemaphoreType.DMA((bins // PER_CHUNK,)),
        ],
        compiler_params=pltpu.CompilerParams(
            collective_id=0, has_side_effects=True, vmem_limit_bytes=48 * 1024 * 1024
        ),
        name="exchange",
    )(plan, records, fir_taps[None, :], jnp.asarray(dft_rows(owners)))


def widen_kernel(narrow, out, wide, sems):
    def copy(place):
        return pltpu.make_async_copy(wide.at[place], out.at[place], sems.at[place])

    for place in range(narrow.shape[0]):
        wide[place] = narrow[place].astype(jnp.float32)
        copy(place).start()
    for place in range(narrow.shape[0]):
        copy(place).wait()


def widen(narrow):
    return pl.pallas_call(
        widen_kernel,
        out_shape=jax.ShapeDtypeStruct(narrow.shape, jnp.float32),
        in_specs=[pl.BlockSpec(memory_space=pltpu.VMEM)],
        out_specs=pl.BlockSpec(memory_space=pl.ANY),
        scratch_shapes=[
            pltpu.VMEM(narrow.shape, jnp.float32),
            pltpu.SemaphoreType.DMA((narrow.shape[0],)),
        ],
        compiler_params=pltpu.CompilerParams(vmem_limit_bytes=24 * 1024 * 1024),
        name="widen",
    )(narrow)


def cross_kernel(scale, groups, rows, slots, own, first, second, out):
    half = rows // 2
    depth, channels = own.shape
    held = own[...].astype(jnp.float32).reshape(groups, rows, channels)
    turned = jnp.concatenate([held[:, half:], -held[:, :half]], axis=1)
    turned = turned.astype(jnp.bfloat16).reshape(depth, channels)
    for index, partner in enumerate((first, second)):
        for part, right in enumerate((own[...], turned)):
            product = lax.dot_general(
                partner[...], right, (((0,), (0,)), ((), ())), preferred_element_type=jnp.float32
            )
            out[index, part] = product * scale


def cross_terms(gathered, slots, groups, scale):
    _, bins, depth, channels = gathered.shape
    taken = lambda which: pl.BlockSpec(
        (None, None, depth, channels), lambda m, s: (s[which], m, 0, 0)
    )
    return pl.pallas_call(
        functools.partial(cross_kernel, scale, groups, depth // groups),
        out_shape=jax.ShapeDtypeStruct((bins, ROUNDS, 2, channels, channels), jnp.float32),
        grid_spec=pltpu.PrefetchScalarGridSpec(
            num_scalar_prefetch=1,
            grid=(bins,),
            in_specs=[
                pl.BlockSpec((None, None, depth, channels), lambda m, s: (0, m, 0, 0)),
                taken(0),
                taken(1),
            ],
            out_specs=pl.BlockSpec(
                (None, ROUNDS, 2, channels, channels), lambda m, s: (m, 0, 0, 0, 0)
            ),
        ),
        compiler_params=pltpu.CompilerParams(
            dimension_semantics=("arbitrary",), vmem_limit_bytes=40 * 1024 * 1024
        ),
        name="cross",
    )(slots, gathered, gathered, gathered)


def gather_images(x):
    owners, bins, rows, channels = x.shape
    swapped = lax.all_to_all(x, "win", 0, 0, tiled=True)
    images = [swapped.transpose(1, 0, 2, 3).reshape(bins, owners * rows, channels)]
    for bit_place in range(lax.axis_size("chan").bit_length() - 1):
        images = images + [from_partner(image, "chan", bit_place) for image in images]
    return jnp.stack(images)


def on_device(records, fir_taps, plan):
    channels, samples_here = records.shape
    window_count = samples_here // WL
    owners = lax.axis_size("win")
    chan = lax.axis_index("chan")
    scale = 1.0 / math.sqrt(window_count * owners)
    keys = jnp.bitwise_xor(plan[:, chan], chan)
    if lax.axis_size("chan") == 4:
        return widen(exchange(records, fir_taps, plan, scale))
    whitened = whiten(records, fir_taps)
    gathered = gather_images(
        whitened.reshape(owners, F // owners, 2 * window_count, channels)
    )
    return cross_terms(gathered, keys.astype(jnp.int32), owners, scale)


def solution(mesh):
    placed = (P("chan", "win"), P(), P())
    return jax.shard_map(
        on_device,
        mesh=mesh,
        in_specs=placed,
        out_specs=P("win", None, None, None, "chan"),
        check_vma=False,
    )
```

```python
import functools
import math

import jax
import jax.numpy as jnp
import numpy as np
from jax import lax
from jax.experimental import pallas as pl
from jax.experimental.pallas import tpu as pltpu
from jax.sharding import PartitionSpec as P

WL = 256
F = 64
TAPS = 64
ROUNDS = 2
LEFT = 128
GROUP = 8
PER_CHUNK = 1
LEAD = 2
SETTLE = LEAD + 12
MESH = pl.DeviceIdType.MESH


def shifted(array, axis, by):
    count = lax.axis_size(axis)
    pairs = [(i, i + by) for i in range(count) if 0 <= i + by < count]
    return lax.ppermute(array, axis, pairs)


def from_partner(block, axis, bit):
    count = lax.axis_size(axis)
    route = []
    for low in range(count):
        high = low | 1 << bit
        if high != low and high < count:
            route += [(low, high), (high, low)]
    return lax.ppermute(block, axis, route)


def fir_matrix(fir_taps):
    inputs_at = jnp.arange(WL + TAPS - 1, dtype=jnp.int32)[:, None]
    outputs_at = jnp.arange(WL, dtype=jnp.int32)[None, :]
    tap_number = outputs_at + (TAPS - 1) - inputs_at
    inside = (tap_number >= 0) & (tap_number < TAPS)
    picked = fir_taps[jnp.clip(tap_number, 0, TAPS - 1)]
    return jnp.where(inside, picked, jnp.zeros_like(picked))


def dft_table():
    sample_at = jnp.arange(WL, dtype=jnp.int32)[:, None]
    column_at = jnp.arange(2 * F, dtype=jnp.int32)[None, :]
    bin_number = column_at // 2 + 1
    phases = (sample_at * bin_number % WL).astype(jnp.float32) * (2.0 * math.pi / WL)
    return jnp.where(column_at % 2 == 0, jnp.cos(phases), -jnp.sin(phases))


def split_table(fir_taps):
    table = jnp.dot(fir_matrix(fir_taps), dft_table(), precision=lax.Precision.HIGHEST)
    high = table.astype(jnp.bfloat16)
    low = (table - high.astype(jnp.float32)).astype(jnp.bfloat16)
    return jnp.concatenate([high, low], axis=1)


def whiten(records, fir_taps):
    channels, samples_here = records.shape
    window_count = samples_here // WL
    previous_tail = shifted(records[:, samples_here - TAPS + 1 :], "win", 1)
    samples = records.reshape(channels, window_count, WL)
    previous = jnp.concatenate(
        [previous_tail[:, None, :], samples[:, :-1, WL - TAPS + 1 :]], axis=1
    )
    table = split_table(fir_taps)
    both = jnp.einsum(
        "cwi,ik->kwc", samples, table[TAPS - 1 :], preferred_element_type=jnp.float32
    )
    both = both + jnp.einsum(
        "cwi,ik->kwc", previous, table[: TAPS - 1], preferred_element_type=jnp.float32
    )
    stacked = both[: 2 * F] + both[2 * F :]
    band_power = jnp.mean(stacked * stacked, axis=0, keepdims=True) + 1e-06
    return (stacked / jnp.sqrt(band_power)).astype(jnp.bfloat16)


def dft_rows(owners):
    bins = F // owners
    place = np.arange(bins)[:, None, None]
    owner = np.arange(owners)[None, :, None]
    part = np.arange(2)[None, None, :]
    number = np.broadcast_to(owner * bins + place + 1, (bins, owners, 2)).reshape(-1, 1)
    part = np.broadcast_to(part, (bins, owners, 2)).reshape(-1, 1)
    phases = (np.arange(WL)[None, :] * number % WL) * (2.0 * np.pi / WL)
    return np.where(part == 0, np.cos(phases), -np.sin(phases)).astype(np.float32)


def exchange_kernel(owners, bins, windows, scale, plan_at, records, taps, dft, out,
                    plan, rec, table, halo, spectra, x, own, recv, stage, acc, result,
                    plan_sem, rec_sem, halo_send, halo_recv, a2a_send, a2a_recv, z_send, z_recv, out_sem):
    chan = lax.axis_index("chan")
    me = lax.axis_index("win")
    is_mid = jnp.logical_and(chan >= 1, chan <= 2)
    is_end = jnp.logical_not(is_mid)
    inner = 3 - chan
    outer = 3 * (chan - 1)
    next_in = 1 + chan // 3
    kept = 2 * F
    lanes = spectra.shape[0] // 2
    groups = windows // GROUP
    pairs = bins // PER_CHUNK
    chunks = groups * pairs
    span = GROUP * WL
    unit = 2 * GROUP

    def load(g):
        columns = pl.ds(pl.multiple_of(g * span, span), span)
        return pltpu.make_async_copy(records.at[:, columns], rec.at[:, columns], rec_sem.at[g])

    plan_copy = pltpu.make_async_copy(plan_at, plan, plan_sem)
    plan_copy.start()
    for g in range(groups):
        load(g).start()

    barrier = pltpu.get_barrier_semaphore()
    for step in range(1, owners):
        pl.semaphore_signal(barrier, inc=1, device_id={"win": lax.rem(me + step, owners)}, device_id_type=MESH)

    @pl.when(is_mid)
    def _():
        pl.semaphore_signal(barrier, inc=1, device_id={"chan": inner}, device_id_type=MESH)
        pl.semaphore_signal(barrier, inc=1, device_id={"chan": outer}, device_id_type=MESH)

    @pl.when(is_end)
    def _():
        pl.semaphore_signal(barrier, inc=1, device_id={"chan": next_in}, device_id_type=MESH)

    row = jnp.concatenate([taps[...], jnp.zeros((1, LEFT + WL + LEFT - TAPS), jnp.float32)], axis=1)
    spread = jnp.broadcast_to(row, (LEFT + WL, LEFT + WL + LEFT))
    shifted_taps = pltpu.roll(spread, 0, 1, stride=1, stride_axis=0)[:, LEFT : LEFT + WL]
    combined = lax.dot_general(
        dft[...], shifted_taps, (((1,), (1,)), ((), ())),
        precision=lax.Precision.HIGHEST, preferred_element_type=jnp.float32,
    )
    high = combined.astype(jnp.bfloat16)
    table[:kept] = high
    table[kept:] = (combined - high.astype(jnp.float32)).astype(jnp.bfloat16)

    def whiten_window(turn, place, segment):
        both = lax.dot_general(
            table[...], segment, (((1,), (1,)), ((), ())), preferred_element_type=jnp.float32
        )
        stacked = both[:kept] + both[kept:]
        power = jnp.mean(stacked * stacked, axis=0, keepdims=True) + 1e-06
        whitened = stacked * (1.0 / jnp.sqrt(power))
        for lane in range(lanes):
            rows = pl.ds(pl.multiple_of(place * kept, kept), kept)
            spectra[lax.rem(turn, 2) * lanes + lane, rows] = whitened[
                :, lane * 128 : lane * 128 + 128
            ]

    def whiten_ahead(step):
        turn, place = step // GROUP, lax.rem(step, GROUP)
        g = lax.rem(turn + 1, groups)
        w = g * GROUP + place

        @pl.when(jnp.logical_and(place == 0, g > 0))
        def _():
            load(g).wait()

        @pl.when(w > 0)
        def _():
            start = pl.multiple_of(w * WL - LEFT, LEFT)
            whiten_window(turn, place, rec[:, pl.ds(start, LEFT + WL)])

        @pl.when(jnp.logical_and(w == 0, me == 0))
        def _():
            halo[...] = jnp.zeros_like(halo)

        @pl.when(jnp.logical_and(w == 0, me > 0))
        def _():
            pltpu.make_async_copy(halo, halo, halo_recv).wait()

        @pl.when(w == 0)
        def _():
            whiten_window(turn, place, jnp.concatenate([halo[...], rec[:, :WL]], axis=1))

    load(0).wait()
    load(1).wait()
    for place in range(GROUP):
        start = span + place * WL - LEFT
        whiten_window(0, place, rec[:, start : start + LEFT + WL])
    pl.semaphore_wait(barrier, jnp.where(is_mid, owners + 1, owners))

    def tail_copy():
        return pltpu.make_async_remote_copy(
            src_ref=records.at[:, pl.ds(windows * WL - LEFT, LEFT)], dst_ref=halo,
            send_sem=halo_send, recv_sem=halo_recv,
            device_id={"win": lax.rem(me + 1, owners)}, device_id_type=MESH,
        )

    @pl.when(me < owners - 1)
    def _():
        tail_copy().start()

    mine = pl.ds(pl.multiple_of(me * unit, unit), unit)

    def start_block(n):
        pair = lax.rem(n, pairs)

        half = lax.rem(n // pairs, 2) * lanes
        for b in range(PER_CHUNK):
            for owner in range(owners):
                first = ((pair * PER_CHUNK + b) * owners + owner) * 2
                for lane in range(lanes):
                    real = spectra[half + lane, pl.ds(first, GROUP, stride=kept)]
                    imag = spectra[half + lane, pl.ds(first + 1, GROUP, stride=kept)]
                    x[n, owner, b, :, lane * 128 : lane * 128 + 128] = jnp.concatenate(
                        [real, imag], axis=0
                    ).astype(jnp.bfloat16)
        for step in range(1, owners):
            target = lax.rem(me + step, owners)
            pltpu.make_async_remote_copy(
                src_ref=x.at[n, target], dst_ref=own.at[n, :, mine],
                send_sem=a2a_send.at[n], recv_sem=a2a_recv.at[n],
                device_id={"win": target}, device_id_type=MESH,
            ).start()
        own[n, :, mine] = x[n, me]

    others = pl.ds(0, (owners - 1) * unit)

    def arrived(n):
        pltpu.make_async_copy(own.at[n, :, others], own.at[n, :, others], a2a_recv.at[n]).wait()

    def along(source, slot, n, which, target):
        return pltpu.make_async_remote_copy(
            src_ref=source.at[n], dst_ref=recv.at[slot, n],
            send_sem=z_send.at[which, n], recv_sem=z_recv.at[slot, n],
            device_id={"chan": target}, device_id_type=MESH,
        )

    def got(slot, n):
        pltpu.make_async_copy(recv.at[slot, n], recv.at[slot, n], z_recv.at[slot, n]).wait()

    def flush(pair):
        place = pl.ds(pair * PER_CHUNK, PER_CHUNK)
        return pltpu.make_async_copy(result.at[place], out.at[place], out_sem.at[pair])

    def multiply(n, choose):
        pair = lax.rem(n, pairs)
        started = n >= pairs
        for b in range(PER_CHUNK):
            at = pair * PER_CHUNK + b
            mine_now = own[n, b]
            depth, channels = mine_now.shape
            held = mine_now.astype(jnp.float32).reshape(owners, unit, channels)
            turned = jnp.concatenate([held[:, GROUP:], -held[:, :GROUP]], axis=1)
            turned = turned.astype(jnp.bfloat16).reshape(depth, channels)
            for index in range(ROUNDS):
                partner = choose(index, b)
                for part, right in enumerate((mine_now, turned)):
                    product = lax.dot_general(
                        partner, right, (((0,), (0,)), ((), ())),
                        preferred_element_type=jnp.float32,
                    )
                    total = jnp.where(started, acc[at, index, part], 0.0) + product
                    acc[at, index, part] = total
                    result[at, index, part] = (total * scale).astype(result.dtype)

        @pl.when(n >= chunks - pairs)
        def _():
            flush(pair).start()

    def when_in(step, lag, body):
        n = step - lag

        @pl.when(jnp.logical_and(n >= 0, n < chunks))
        def _():
            body(n)

    def when_ahead(step):
        @pl.when(step < chunks - pairs)
        def _():
            whiten_ahead(step + GROUP)

    def sent(n):
        pltpu.make_async_copy(own.at[n, :, others], own.at[n, :, others], a2a_send.at[n]).wait()

    def run(steps, body, finish):
        lax.fori_loop(0, steps, body, 0)

        def rest(n, carry):
            finish(n)
            return carry

        lax.fori_loop(steps - SETTLE, chunks, rest, 0)

    plan_copy.wait()
    keys = [plan[index, 0] for index in range(ROUNDS)]
    has_1 = jnp.logical_or(keys[0] == 1, keys[1] == 1)
    has_3 = jnp.logical_or(keys[0] == 3, keys[1] == 3)

    @pl.when(is_mid)
    def _():
        def take_own(n):
            arrived(n)
            along(own, 1, n, 0, inner).start()

        def take_outer(n):
            got(0, n)
            along(recv.at[0], 2, n, 1, inner).start()

        def take_inner(n):
            got(1, n)
            stage[0, n] = jnp.where(has_1, own[n], recv[1, n])
            along(stage.at[0], 0, n, 2, outer).start()

        def take_far(n):
            got(2, n)
            stage[1, n] = jnp.where(has_3, recv[2, n], recv[1, n])
            along(stage.at[1], 1, n, 3, outer).start()

        def multiply_mid(n):
            def choose(index, b):
                key = keys[index]
                later = jnp.where(key == 3, recv[1, n, b], recv[2, n, b])
                return jnp.where(key == 1, recv[0, n, b], later)

            multiply(n, choose)

        def finish(n):
            sent(n)
            along(own, 1, n, 0, inner).wait_send()
            along(recv.at[0], 2, n, 1, inner).wait_send()
            along(stage.at[0], 0, n, 2, outer).wait_send()
            along(stage.at[1], 1, n, 3, outer).wait_send()

        def step_mid(step, carry):
            when_in(step, LEAD, take_own)
            when_in(step, LEAD + 2, take_inner)
            when_in(step, LEAD + 2, take_outer)
            when_in(step, LEAD + 4, take_far)
            when_in(step, 0, start_block)
            when_in(step, LEAD + 4, multiply_mid)
            when_in(step, SETTLE, finish)
            when_ahead(step)
            return carry

        run(chunks + LEAD + 4, step_mid, finish)

    @pl.when(is_end)
    def _():
        def take_own(n):
            arrived(n)
            along(own, 0, n, 0, next_in).start()

        def take_both(n):
            got(0, n)
            got(1, n)

            def choose(index, b):
                key = keys[index]
                in_first = jnp.logical_or(
                    key == 1, jnp.logical_and(key == 2, jnp.logical_not(has_1))
                )
                return jnp.where(in_first, recv[0, n, b], recv[1, n, b])

            multiply(n, choose)

        def finish(n):
            sent(n)
            along(own, 0, n, 0, next_in).wait_send()

        def step_end(step, carry):
            when_in(step, LEAD, take_own)
            when_in(step, 0, start_block)
            when_in(step, SETTLE, finish)
            when_in(step, LEAD + 7, take_both)
            when_ahead(step)
            return carry

        run(chunks + LEAD + 7, step_end, finish)


    for pair in range(pairs):
        flush(pair).wait()

    @pl.when(me < owners - 1)
    def _():
        tail_copy().wait_send()


def exchange(records, fir_taps, plan, scale):
    channels, samples_here = records.shape
    owners = lax.axis_size("win")
    bins, windows = F // owners, samples_here // WL
    chunks = (windows // GROUP) * (bins // PER_CHUNK)
    block = (chunks, PER_CHUNK, owners * 2 * GROUP, channels)
    in_place = pl.BlockSpec(memory_space=pl.ANY)
    in_vmem = pl.BlockSpec(memory_space=pltpu.VMEM)
    result = (bins, ROUNDS, 2, channels, channels)
    return pl.pallas_call(
        functools.partial(exchange_kernel, owners, bins, windows, scale),
        out_shape=jax.ShapeDtypeStruct(result, jnp.bfloat16),
        in_specs=[in_place, in_place, in_vmem, in_vmem],
        out_specs=in_place,
        scratch_shapes=[
            pltpu.SMEM(plan.shape, jnp.int32),
            pltpu.VMEM(records.shape, jnp.bfloat16),
            pltpu.VMEM((4 * F, LEFT + WL), jnp.bfloat16),
            pltpu.VMEM((channels, LEFT), jnp.bfloat16),
            pltpu.VMEM((channels // 128 * 2, GROUP * 2 * F, 128), jnp.float32),
            pltpu.VMEM((chunks, owners, PER_CHUNK, 2 * GROUP, channels), jnp.bfloat16),
            pltpu.VMEM(block, jnp.bfloat16),
            pltpu.VMEM((3,) + block, jnp.bfloat16),
            pltpu.VMEM((2,) + block, jnp.bfloat16),
            pltpu.VMEM(result, jnp.float32),
            pltpu.VMEM(result, jnp.bfloat16),
            pltpu.SemaphoreType.DMA,
            pltpu.SemaphoreType.DMA((windows // GROUP,)),
            pltpu.SemaphoreType.DMA,
            pltpu.SemaphoreType.DMA,
            pltpu.SemaphoreType.DMA((chunks,)),
            pltpu.SemaphoreType.DMA((chunks,)),
            pltpu.SemaphoreType.DMA((4, chunks)),
            pltpu.SemaphoreType.DMA((3, chunks)),
            pltpu.SemaphoreType.DMA((bins // PER_CHUNK,)),
        ],
        compiler_params=pltpu.CompilerParams(
            collective_id=0, has_side_effects=True, vmem_limit_bytes=48 * 1024 * 1024
        ),
        name="exchange",
    )(plan, records, fir_taps[None, :], jnp.asarray(dft_rows(owners)))


def widen_kernel(narrow, out, wide, sems):
    def copy(place):
        return pltpu.make_async_copy(wide.at[place], out.at[place], sems.at[place])

    for place in range(narrow.shape[0]):
        wide[place] = narrow[place].astype(jnp.float32)
        copy(place).start()
    for place in range(narrow.shape[0]):
        copy(place).wait()


def widen(narrow):
    return pl.pallas_call(
        widen_kernel,
        out_shape=jax.ShapeDtypeStruct(narrow.shape, jnp.float32),
        in_specs=[pl.BlockSpec(memory_space=pltpu.VMEM)],
        out_specs=pl.BlockSpec(memory_space=pl.ANY),
        scratch_shapes=[
            pltpu.VMEM(narrow.shape, jnp.float32),
            pltpu.SemaphoreType.DMA((narrow.shape[0],)),
        ],
        compiler_params=pltpu.CompilerParams(vmem_limit_bytes=24 * 1024 * 1024),
        name="widen",
    )(narrow)


def cross_kernel(scale, groups, rows, slots, own, first, second, out):
    half = rows // 2
    depth, channels = own.shape
    held = own[...].astype(jnp.float32).reshape(groups, rows, channels)
    turned = jnp.concatenate([held[:, half:], -held[:, :half]], axis=1)
    turned = turned.astype(jnp.bfloat16).reshape(depth, channels)
    for index, partner in enumerate((first, second)):
        for part, right in enumerate((own[...], turned)):
            product = lax.dot_general(
                partner[...], right, (((0,), (0,)), ((), ())), preferred_element_type=jnp.float32
            )
            out[index, part] = product * scale


def cross_terms(gathered, slots, groups, scale):
    _, bins, depth, channels = gathered.shape
    taken = lambda which: pl.BlockSpec(
        (None, None, depth, channels), lambda m, s: (s[which], m, 0, 0)
    )
    return pl.pallas_call(
        functools.partial(cross_kernel, scale, groups, depth // groups),
        out_shape=jax.ShapeDtypeStruct((bins, ROUNDS, 2, channels, channels), jnp.float32),
        grid_spec=pltpu.PrefetchScalarGridSpec(
            num_scalar_prefetch=1,
            grid=(bins,),
            in_specs=[
                pl.BlockSpec((None, None, depth, channels), lambda m, s: (0, m, 0, 0)),
                taken(0),
                taken(1),
            ],
            out_specs=pl.BlockSpec(
                (None, ROUNDS, 2, channels, channels), lambda m, s: (m, 0, 0, 0, 0)
            ),
        ),
        compiler_params=pltpu.CompilerParams(
            dimension_semantics=("arbitrary",), vmem_limit_bytes=40 * 1024 * 1024
        ),
        name="cross",
    )(slots, gathered, gathered, gathered)


def gather_images(x):
    owners, bins, rows, channels = x.shape
    swapped = lax.all_to_all(x, "win", 0, 0, tiled=True)
    images = [swapped.transpose(1, 0, 2, 3).reshape(bins, owners * rows, channels)]
    for bit_place in range(lax.axis_size("chan").bit_length() - 1):
        images = images + [from_partner(image, "chan", bit_place) for image in images]
    return jnp.stack(images)


def on_device(records, fir_taps, plan):
    channels, samples_here = records.shape
    window_count = samples_here // WL
    owners = lax.axis_size("win")
    chan = lax.axis_index("chan")
    scale = 1.0 / math.sqrt(window_count * owners)
    keys = jnp.bitwise_xor(plan[:, chan], chan)
    if lax.axis_size("chan") == 4 and F // owners == GROUP * PER_CHUNK:
        return widen(exchange(records, fir_taps, plan, scale))
    whitened = whiten(records, fir_taps)
    gathered = gather_images(
        whitened.reshape(owners, F // owners, 2 * window_count, channels)
    )
    return cross_terms(gathered, keys.astype(jnp.int32), owners, scale)


def solution(mesh):
    placed = (P("chan", "win"), P(), P())
    return jax.shard_map(
        on_device,
        mesh=mesh,
        in_specs=placed,
        out_specs=P("win", None, None, None, "chan"),
        check_vma=False,
    )
```

```python
import functools
import math

import jax
import jax.numpy as jnp
import numpy as np
from jax import lax
from jax.experimental import pallas as pl
from jax.experimental.pallas import tpu as pltpu
from jax.sharding import PartitionSpec as P

WL = 256
F = 64
TAPS = 64
ROUNDS = 2
LEFT = 128
GROUP = 8
PER_CHUNK = 1
LEAD = 2
SETTLE = LEAD + 12
MESH = pl.DeviceIdType.MESH


def shifted(array, axis, by):
    count = lax.axis_size(axis)
    pairs = [(i, i + by) for i in range(count) if 0 <= i + by < count]
    return lax.ppermute(array, axis, pairs)


def from_partner(block, axis, bit):
    count = lax.axis_size(axis)
    route = []
    for low in range(count):
        high = low | 1 << bit
        if high != low and high < count:
            route += [(low, high), (high, low)]
    return lax.ppermute(block, axis, route)


def fir_matrix(fir_taps):
    inputs_at = jnp.arange(WL + TAPS - 1, dtype=jnp.int32)[:, None]
    outputs_at = jnp.arange(WL, dtype=jnp.int32)[None, :]
    tap_number = outputs_at + (TAPS - 1) - inputs_at
    inside = (tap_number >= 0) & (tap_number < TAPS)
    picked = fir_taps[jnp.clip(tap_number, 0, TAPS - 1)]
    return jnp.where(inside, picked, jnp.zeros_like(picked))


def dft_table():
    sample_at = jnp.arange(WL, dtype=jnp.int32)[:, None]
    column_at = jnp.arange(2 * F, dtype=jnp.int32)[None, :]
    bin_number = column_at // 2 + 1
    phases = (sample_at * bin_number % WL).astype(jnp.float32) * (2.0 * math.pi / WL)
    return jnp.where(column_at % 2 == 0, jnp.cos(phases), -jnp.sin(phases))


def split_table(fir_taps):
    table = jnp.dot(fir_matrix(fir_taps), dft_table(), precision=lax.Precision.HIGHEST)
    high = table.astype(jnp.bfloat16)
    low = (table - high.astype(jnp.float32)).astype(jnp.bfloat16)
    return jnp.concatenate([high, low], axis=1)


def whiten(records, fir_taps):
    channels, samples_here = records.shape
    window_count = samples_here // WL
    previous_tail = shifted(records[:, samples_here - TAPS + 1 :], "win", 1)
    samples = records.reshape(channels, window_count, WL)
    previous = jnp.concatenate(
        [previous_tail[:, None, :], samples[:, :-1, WL - TAPS + 1 :]], axis=1
    )
    table = split_table(fir_taps)
    both = jnp.einsum(
        "cwi,ik->kwc", samples, table[TAPS - 1 :], preferred_element_type=jnp.float32
    )
    both = both + jnp.einsum(
        "cwi,ik->kwc", previous, table[: TAPS - 1], preferred_element_type=jnp.float32
    )
    stacked = both[: 2 * F] + both[2 * F :]
    band_power = jnp.mean(stacked * stacked, axis=0, keepdims=True) + 1e-06
    return (stacked / jnp.sqrt(band_power)).astype(jnp.bfloat16)


def dft_rows(owners):
    bins = F // owners
    place = np.arange(bins)[:, None, None]
    owner = np.arange(owners)[None, :, None]
    part = np.arange(2)[None, None, :]
    number = np.broadcast_to(owner * bins + place + 1, (bins, owners, 2)).reshape(-1, 1)
    part = np.broadcast_to(part, (bins, owners, 2)).reshape(-1, 1)
    phases = (np.arange(WL)[None, :] * number % WL) * (2.0 * np.pi / WL)
    return np.where(part == 0, np.cos(phases), -np.sin(phases)).astype(np.float32)


def exchange_kernel(owners, bins, windows, scale, plan_at, records, taps, dft, out,
                    plan, rec, table, halo, spectra, x, own, recv, stage, acc, result,
                    plan_sem, rec_sem, halo_send, halo_recv, a2a_send, a2a_recv, z_send, z_recv, out_sem):
    chan = lax.axis_index("chan")
    me = lax.axis_index("win")
    is_mid = jnp.logical_and(chan >= 1, chan <= 2)
    is_end = jnp.logical_not(is_mid)
    inner = 3 - chan
    outer = 3 * (chan - 1)
    next_in = 1 + chan // 3
    kept = 2 * F
    lanes = spectra.shape[0] // 2
    groups = windows // GROUP
    pairs = bins // PER_CHUNK
    chunks = groups * pairs
    span = GROUP * WL
    unit = 2 * GROUP

    def load(g):
        columns = pl.ds(pl.multiple_of(g * span, span), span)
        return pltpu.make_async_copy(records.at[:, columns], rec.at[:, columns], rec_sem.at[g])

    plan_copy = pltpu.make_async_copy(plan_at, plan, plan_sem)
    plan_copy.start()
    for g in range(groups):
        load(g).start()

    barrier = pltpu.get_barrier_semaphore()
    for step in range(1, owners):
        pl.semaphore_signal(barrier, inc=1, device_id={"win": lax.rem(me + step, owners)}, device_id_type=MESH)

    @pl.when(is_mid)
    def _():
        pl.semaphore_signal(barrier, inc=1, device_id={"chan": inner}, device_id_type=MESH)
        pl.semaphore_signal(barrier, inc=1, device_id={"chan": outer}, device_id_type=MESH)

    @pl.when(is_end)
    def _():
        pl.semaphore_signal(barrier, inc=1, device_id={"chan": next_in}, device_id_type=MESH)

    row = jnp.concatenate([taps[...], jnp.zeros((1, LEFT + WL + LEFT - TAPS), jnp.float32)], axis=1)
    spread = jnp.broadcast_to(row, (LEFT + WL, LEFT + WL + LEFT))
    shifted_taps = pltpu.roll(spread, 0, 1, stride=1, stride_axis=0)[:, LEFT : LEFT + WL]
    combined = lax.dot_general(
        dft[...], shifted_taps, (((1,), (1,)), ((), ())),
        precision=lax.Precision.HIGHEST, preferred_element_type=jnp.float32,
    )
    high = combined.astype(jnp.bfloat16)
    table[:kept] = high
    table[kept:] = (combined - high.astype(jnp.float32)).astype(jnp.bfloat16)

    def whiten_window(turn, place, segment):
        both = lax.dot_general(
            table[...], segment, (((1,), (1,)), ((), ())), preferred_element_type=jnp.float32
        )
        stacked = both[:kept] + both[kept:]
        power = jnp.mean(stacked * stacked, axis=0, keepdims=True) + 1e-06
        whitened = stacked * (1.0 / jnp.sqrt(power))
        for lane in range(lanes):
            rows = pl.ds(pl.multiple_of(place * kept, kept), kept)
            spectra[lax.rem(turn, 2) * lanes + lane, rows] = whitened[
                :, lane * 128 : lane * 128 + 128
            ]

    def whiten_ahead(step):
        turn, place = step // GROUP, lax.rem(step, GROUP)
        g = lax.rem(turn + 1, groups)
        w = g * GROUP + place

        @pl.when(jnp.logical_and(place == 0, g > 0))
        def _():
            load(g).wait()

        @pl.when(w > 0)
        def _():
            start = pl.multiple_of(w * WL - LEFT, LEFT)
            whiten_window(turn, place, rec[:, pl.ds(start, LEFT + WL)])

        @pl.when(jnp.logical_and(w == 0, me == 0))
        def _():
            halo[...] = jnp.zeros_like(halo)

        @pl.when(jnp.logical_and(w == 0, me > 0))
        def _():
            pltpu.make_async_copy(halo, halo, halo_recv).wait()

        @pl.when(w == 0)
        def _():
            whiten_window(turn, place, jnp.concatenate([halo[...], rec[:, :WL]], axis=1))

    load(0).wait()
    load(1).wait()
    for place in range(GROUP):
        start = span + place * WL - LEFT
        whiten_window(0, place, rec[:, start : start + LEFT + WL])
    pl.semaphore_wait(barrier, jnp.where(is_mid, owners + 1, owners))

    def tail_copy():
        return pltpu.make_async_remote_copy(
            src_ref=records.at[:, pl.ds(windows * WL - LEFT, LEFT)], dst_ref=halo,
            send_sem=halo_send, recv_sem=halo_recv,
            device_id={"win": lax.rem(me + 1, owners)}, device_id_type=MESH,
        )

    @pl.when(me < owners - 1)
    def _():
        tail_copy().start()

    mine = pl.ds(pl.multiple_of(me * unit, unit), unit)

    def start_block(n):
        pair = lax.rem(n, pairs)

        half = lax.rem(n // pairs, 2) * lanes
        for b in range(PER_CHUNK):
            for owner in range(owners):
                first = ((pair * PER_CHUNK + b) * owners + owner) * 2
                for lane in range(lanes):
                    real = spectra[half + lane, pl.ds(first, GROUP, stride=kept)]
                    imag = spectra[half + lane, pl.ds(first + 1, GROUP, stride=kept)]
                    x[n, owner, b, :, lane * 128 : lane * 128 + 128] = jnp.concatenate(
                        [real, imag], axis=0
                    ).astype(jnp.bfloat16)
        for step in range(1, owners):
            target = lax.rem(me + step, owners)
            pltpu.make_async_remote_copy(
                src_ref=x.at[n, target], dst_ref=own.at[n, :, mine],
                send_sem=a2a_send.at[n], recv_sem=a2a_recv.at[n],
                device_id={"win": target}, device_id_type=MESH,
            ).start()
        own[n, :, mine] = x[n, me]

    others = pl.ds(0, (owners - 1) * unit)

    def arrived(n):
        pltpu.make_async_copy(own.at[n, :, others], own.at[n, :, others], a2a_recv.at[n]).wait()

    def along(source, slot, n, which, target):
        return pltpu.make_async_remote_copy(
            src_ref=source.at[n], dst_ref=recv.at[slot, n],
            send_sem=z_send.at[which, n], recv_sem=z_recv.at[slot, n],
            device_id={"chan": target}, device_id_type=MESH,
        )

    def got(slot, n):
        pltpu.make_async_copy(recv.at[slot, n], recv.at[slot, n], z_recv.at[slot, n]).wait()

    def flush(pair):
        place = pl.ds(pair * PER_CHUNK, PER_CHUNK)
        return pltpu.make_async_copy(result.at[place], out.at[place], out_sem.at[pair])

    def multiply(n, choose):
        pair = lax.rem(n, pairs)
        started = n >= pairs
        for b in range(PER_CHUNK):
            at = pair * PER_CHUNK + b
            mine_now = own[n, b]
            depth, channels = mine_now.shape
            held = mine_now.astype(jnp.float32).reshape(owners, unit, channels)
            turned = jnp.concatenate([held[:, GROUP:], -held[:, :GROUP]], axis=1)
            turned = turned.astype(jnp.bfloat16).reshape(depth, channels)
            for index in range(ROUNDS):
                partner = choose(index, b)
                for part, right in enumerate((mine_now, turned)):
                    product = lax.dot_general(
                        partner, right, (((0,), (0,)), ((), ())),
                        preferred_element_type=jnp.float32,
                    )
                    total = jnp.where(started, acc[at, index, part], 0.0) + product
                    acc[at, index, part] = total
                    result[at, index, part] = (total * scale).astype(result.dtype)

        @pl.when(n >= chunks - pairs)
        def _():
            flush(pair).start()

    def when_in(step, lag, body):
        n = step - lag

        @pl.when(jnp.logical_and(n >= 0, n < chunks))
        def _():
            body(n)

    def when_ahead(step):
        @pl.when(step < chunks - pairs)
        def _():
            whiten_ahead(step + GROUP)

    def sent(n):
        pltpu.make_async_copy(own.at[n, :, others], own.at[n, :, others], a2a_send.at[n]).wait()

    def run(steps, body, finish):
        lax.fori_loop(0, steps, body, 0)

        def rest(n, carry):
            finish(n)
            return carry

        lax.fori_loop(steps - SETTLE, chunks, rest, 0)

    plan_copy.wait()
    keys = [plan[index, 0] for index in range(ROUNDS)]
    has_1 = jnp.logical_or(keys[0] == 1, keys[1] == 1)
    has_3 = jnp.logical_or(keys[0] == 3, keys[1] == 3)

    @pl.when(is_mid)
    def _():
        def take_own(n):
            arrived(n)
            along(own, 1, n, 0, inner).start()

        def take_outer(n):
            got(0, n)
            along(recv.at[0], 2, n, 1, inner).start()

        def take_inner(n):
            got(1, n)
            stage[0, n] = jnp.where(has_1, own[n], recv[1, n])
            along(stage.at[0], 0, n, 2, outer).start()

        def take_far(n):
            got(2, n)
            stage[1, n] = jnp.where(has_3, recv[2, n], recv[1, n])
            along(stage.at[1], 1, n, 3, outer).start()

        def multiply_mid(n):
            def choose(index, b):
                key = keys[index]
                later = jnp.where(key == 3, recv[1, n, b], recv[2, n, b])
                return jnp.where(key == 1, recv[0, n, b], later)

            multiply(n, choose)

        def finish(n):
            sent(n)
            along(own, 1, n, 0, inner).wait_send()
            along(recv.at[0], 2, n, 1, inner).wait_send()
            along(stage.at[0], 0, n, 2, outer).wait_send()
            along(stage.at[1], 1, n, 3, outer).wait_send()

        def step_mid(step, carry):
            when_in(step, LEAD, take_own)
            when_in(step, LEAD + 1, take_inner)
            when_in(step, LEAD + 2, take_outer)
            when_in(step, LEAD + 3, take_far)
            when_in(step, 0, start_block)
            when_in(step, LEAD + 3, multiply_mid)
            when_in(step, SETTLE, finish)
            when_ahead(step)
            return carry

        run(chunks + LEAD + 3, step_mid, finish)

    @pl.when(is_end)
    def _():
        def take_own(n):
            arrived(n)
            along(own, 0, n, 0, next_in).start()

        def take_both(n):
            got(0, n)
            got(1, n)

            def choose(index, b):
                key = keys[index]
                in_first = jnp.logical_or(
                    key == 1, jnp.logical_and(key == 2, jnp.logical_not(has_1))
                )
                return jnp.where(in_first, recv[0, n, b], recv[1, n, b])

            multiply(n, choose)

        def finish(n):
            sent(n)
            along(own, 0, n, 0, next_in).wait_send()

        def step_end(step, carry):
            when_in(step, LEAD, take_own)
            when_in(step, 0, start_block)
            when_in(step, SETTLE, finish)
            when_in(step, LEAD + 7, take_both)
            when_ahead(step)
            return carry

        run(chunks + LEAD + 7, step_end, finish)


    for pair in range(pairs):
        flush(pair).wait()

    @pl.when(me < owners - 1)
    def _():
        tail_copy().wait_send()


def exchange(records, fir_taps, plan, scale):
    channels, samples_here = records.shape
    owners = lax.axis_size("win")
    bins, windows = F // owners, samples_here // WL
    chunks = (windows // GROUP) * (bins // PER_CHUNK)
    block = (chunks, PER_CHUNK, owners * 2 * GROUP, channels)
    in_place = pl.BlockSpec(memory_space=pl.ANY)
    in_vmem = pl.BlockSpec(memory_space=pltpu.VMEM)
    result = (bins, ROUNDS, 2, channels, channels)
    return pl.pallas_call(
        functools.partial(exchange_kernel, owners, bins, windows, scale),
        out_shape=jax.ShapeDtypeStruct(result, jnp.bfloat16),
        in_specs=[in_place, in_place, in_vmem, in_vmem],
        out_specs=in_place,
        scratch_shapes=[
            pltpu.SMEM(plan.shape, jnp.int32),
            pltpu.VMEM(records.shape, jnp.bfloat16),
            pltpu.VMEM((4 * F, LEFT + WL), jnp.bfloat16),
            pltpu.VMEM((channels, LEFT), jnp.bfloat16),
            pltpu.VMEM((channels // 128 * 2, GROUP * 2 * F, 128), jnp.float32),
            pltpu.VMEM((chunks, owners, PER_CHUNK, 2 * GROUP, channels), jnp.bfloat16),
            pltpu.VMEM(block, jnp.bfloat16),
            pltpu.VMEM((3,) + block, jnp.bfloat16),
            pltpu.VMEM((2,) + block, jnp.bfloat16),
            pltpu.VMEM(result, jnp.float32),
            pltpu.VMEM(result, jnp.bfloat16),
            pltpu.SemaphoreType.DMA,
            pltpu.SemaphoreType.DMA((windows // GROUP,)),
            pltpu.SemaphoreType.DMA,
            pltpu.SemaphoreType.DMA,
            pltpu.SemaphoreType.DMA((chunks,)),
            pltpu.SemaphoreType.DMA((chunks,)),
            pltpu.SemaphoreType.DMA((4, chunks)),
            pltpu.SemaphoreType.DMA((3, chunks)),
            pltpu.SemaphoreType.DMA((bins // PER_CHUNK,)),
        ],
        compiler_params=pltpu.CompilerParams(
            collective_id=0, has_side_effects=True, vmem_limit_bytes=48 * 1024 * 1024
        ),
        name="exchange",
    )(plan, records, fir_taps[None, :], jnp.asarray(dft_rows(owners)))


def widen_kernel(narrow, out, wide, sems):
    def copy(place):
        return pltpu.make_async_copy(wide.at[place], out.at[place], sems.at[place])

    for place in range(narrow.shape[0]):
        wide[place] = narrow[place].astype(jnp.float32)
        copy(place).start()
    for place in range(narrow.shape[0]):
        copy(place).wait()


def widen(narrow):
    return pl.pallas_call(
        widen_kernel,
        out_shape=jax.ShapeDtypeStruct(narrow.shape, jnp.float32),
        in_specs=[pl.BlockSpec(memory_space=pltpu.VMEM)],
        out_specs=pl.BlockSpec(memory_space=pl.ANY),
        scratch_shapes=[
            pltpu.VMEM(narrow.shape, jnp.float32),
            pltpu.SemaphoreType.DMA((narrow.shape[0],)),
        ],
        compiler_params=pltpu.CompilerParams(vmem_limit_bytes=24 * 1024 * 1024),
        name="widen",
    )(narrow)


def cross_kernel(scale, groups, rows, slots, own, first, second, out):
    half = rows // 2
    depth, channels = own.shape
    held = own[...].astype(jnp.float32).reshape(groups, rows, channels)
    turned = jnp.concatenate([held[:, half:], -held[:, :half]], axis=1)
    turned = turned.astype(jnp.bfloat16).reshape(depth, channels)
    for index, partner in enumerate((first, second)):
        for part, right in enumerate((own[...], turned)):
            product = lax.dot_general(
                partner[...], right, (((0,), (0,)), ((), ())), preferred_element_type=jnp.float32
            )
            out[index, part] = product * scale


def cross_terms(gathered, slots, groups, scale):
    _, bins, depth, channels = gathered.shape
    taken = lambda which: pl.BlockSpec(
        (None, None, depth, channels), lambda m, s: (s[which], m, 0, 0)
    )
    return pl.pallas_call(
        functools.partial(cross_kernel, scale, groups, depth // groups),
        out_shape=jax.ShapeDtypeStruct((bins, ROUNDS, 2, channels, channels), jnp.float32),
        grid_spec=pltpu.PrefetchScalarGridSpec(
            num_scalar_prefetch=1,
            grid=(bins,),
            in_specs=[
                pl.BlockSpec((None, None, depth, channels), lambda m, s: (0, m, 0, 0)),
                taken(0),
                taken(1),
            ],
            out_specs=pl.BlockSpec(
                (None, ROUNDS, 2, channels, channels), lambda m, s: (m, 0, 0, 0, 0)
            ),
        ),
        compiler_params=pltpu.CompilerParams(
            dimension_semantics=("arbitrary",), vmem_limit_bytes=40 * 1024 * 1024
        ),
        name="cross",
    )(slots, gathered, gathered, gathered)


def gather_images(x):
    owners, bins, rows, channels = x.shape
    swapped = lax.all_to_all(x, "win", 0, 0, tiled=True)
    images = [swapped.transpose(1, 0, 2, 3).reshape(bins, owners * rows, channels)]
    for bit_place in range(lax.axis_size("chan").bit_length() - 1):
        images = images + [from_partner(image, "chan", bit_place) for image in images]
    return jnp.stack(images)


def on_device(records, fir_taps, plan):
    channels, samples_here = records.shape
    window_count = samples_here // WL
    owners = lax.axis_size("win")
    chan = lax.axis_index("chan")
    scale = 1.0 / math.sqrt(window_count * owners)
    keys = jnp.bitwise_xor(plan[:, chan], chan)
    if lax.axis_size("chan") == 4 and F // owners == GROUP * PER_CHUNK:
        return widen(exchange(records, fir_taps, plan, scale))
    whitened = whiten(records, fir_taps)
    gathered = gather_images(
        whitened.reshape(owners, F // owners, 2 * window_count, channels)
    )
    return cross_terms(gathered, keys.astype(jnp.int32), owners, scale)


def solution(mesh):
    placed = (P("chan", "win"), P(), P())
    return jax.shard_map(
        on_device,
        mesh=mesh,
        in_specs=placed,
        out_specs=P("win", None, None, None, "chan"),
        check_vma=False,
    )
```
